32 devices in a mesh: groups: 2 (over x), span: 16 (over z, y, core).
Axes of the slice: x: 2, y: 2, z: 4, core: 2. Of those that a mesh axis runs over, the one named last changes fastest.
Arguments:
- queries: bfloat16 [8192, 1024], P(('groups', 'span')), parts along dimension 0, may hold values from -96 to 96
- keys: bfloat16 [8192, 1024], P(('groups', 'span')), parts along dimension 0, may hold values from -9 to 9
- values: bfloat16 [8192, 1024], P(('groups', 'span')), parts along dimension 0, may hold values from -6 to 6
- track: int32 [64, 16], P(('groups', 'span')), parts along dimension 0, may hold values 0 or 1
- out_weight: bfloat16 [1024, 1024], replicated, may hold values from -0.1875 to 0.1875
- grad_out: bfloat16 [8192, 1024], P(('groups', 'span')), parts along dimension 0, may hold values from -6 to 6
Outputs:
- query_grad: bfloat16 [8192, 1024], P(('groups', 'span')), parts along dimension 0
- key_grad: bfloat16 [8192, 1024], P(('groups', 'span')), parts along dimension 0
- value_grad: bfloat16 [8192, 1024], P(('groups', 'span')), parts along dimension 0
- weight_grad: float32 [2048, 1024], P(('groups', 'span')), parts along dimension 0
The draws below stay inside these ranges and needn't reach their ends.
There are 2 independent parts, one for each index of `groups`. The reference program is written for one: setup_inputs(seed, part) draws one part's arguments, and reference() takes and returns one part's arrays. A program takes and returns all parts, laid end to end along the dimension named above; an argument that names none is the same for every part. Nothing has to cross between parts.
All inputs are finite; a program needn't handle non-finite values. No bound on the sum of `track` on one device may be relied on, other than what follows from the above.
Results may differ from the reference program's by a relative error of at most 0.039.
Values may be sent and summed in bfloat16 or wider, within the bound.
No kernel may reach another device: no remote copies, remote signals or barrier semaphores. Data moves between devices by JAX's collectives and lax.ppermute only.
A program may use at most 64 MiB of HBM per device.

```python
import jax
import jax.numpy as jnp
from jax import lax

D = 1024
HEADS = 16
BLOCK = 128
TOK_DEV = 256
WINDOW = 8
TOKENS = 4096
QBLOCKS = 32
MEMBLOCKS = 16
N_SPAN = 16


def shared_keys(key):
    base = jax.random.fold_in(key, 7)
    raw = jnp.clip(1.5 * jax.random.normal(base, (TOKENS, D), jnp.float32), -9.0, 9.0)
    return raw


def draw_keys(key, part):
    return shared_keys(key).astype(jnp.bfloat16)


def draw_queries(key, part):
    base = jax.random.fold_in(key, 11)
    raw = jnp.clip(1.5 * jax.random.normal(base, (TOKENS, D), jnp.float32), -9.0, 9.0)
    return raw.astype(jnp.bfloat16)


def touch_ends(values, key, smallest, top_value):
    longest = values.shape.index(max(values.shape))
    spots = []
    for shift in (0, 1):
        where = [jax.random.randint(jax.random.fold_in(key, axis), (), 0, length) for axis, length in enumerate(values.shape)]
        where[longest] = (where[longest] + shift) % values.shape[longest]
        spots.append(tuple(where))
    return values.at[spots[0]].set(smallest).at[spots[1]].set(top_value)


def shard_levels(rng, shape, pieces, low, largest):
    factor_of = 1.0
    for dim, parts in pieces:
        steps = jax.random.uniform(jax.random.fold_in(jax.random.fold_in(rng, 6), dim), (parts,), jnp.float32, low / len(pieces), largest / len(pieces))
        factor_of = factor_of * jnp.repeat(jnp.exp(steps), shape[dim] // parts).reshape((-1,) + (1,) * (len(shape) - 1 - dim))
    return factor_of


def noise(key, dims, width, reach, cuts=(), kind=jnp.bfloat16):
    values = jax.random.normal(key, dims, jnp.float32) * width
    if len(cuts) > 0:
        values = shard_levels(key, dims, cuts, -0.22, 0.18) * values
    return jnp.clip(values, min=-reach, max=reach).astype(kind)


def setup_inputs(seed: int = 0, part: int = 0) -> dict:
    streams_of = jax.random.split(jax.random.key(seed), 7)
    part_keys = jax.random.split(jax.random.fold_in(streams_of[6], part), 7)
    return {
        "queries": draw_queries(jax.random.fold_in(jax.random.fold_in(streams_of[6], part), 71), part),
        "keys": draw_keys(jax.random.fold_in(jax.random.fold_in(streams_of[6], part), 71), part),
        "values": noise(part_keys[2], (TOKENS, D), 1.0, 6.0, ((0, 16),)),
        "track": touch_ends((jax.random.randint(part_keys[3], (QBLOCKS, MEMBLOCKS), 0, 2) < 1).astype(jnp.int32), jax.random.fold_in(part_keys[3], 1), 0, 1),
        "out_weight": noise(streams_of[4], (D, D), D ** -0.5, 0.1875),
        "grad_out": noise(part_keys[5], (TOKENS, D), 1.0, 6.0, ((0, 16),)),
    }


def head_grads(query_h, key_h, value_h, grad_h, allowed, local_count):
    scale = query_h.shape[-1] ** -0.5
    scores = jnp.einsum('rd,kd->rk', query_h.astype(jnp.float32), key_h.astype(jnp.float32)) * scale
    scores = jnp.where(allowed, scores, jnp.float32(-1e30))
    top = jnp.max(scores, axis=-1, keepdims=True)
    expo = jnp.exp(scores - top)
    probs = expo / jnp.sum(expo, axis=-1, keepdims=True)
    probs_low = probs.astype(jnp.bfloat16)
    attn = jnp.einsum('rk,kd->rd', probs_low.astype(jnp.float32), value_h.astype(jnp.float32)).astype(jnp.bfloat16)
    delta = jnp.sum(grad_h.astype(jnp.float32) * attn.astype(jnp.float32), axis=-1)
    dprob = jnp.einsum('rd,kd->rk', grad_h.astype(jnp.float32), value_h.astype(jnp.float32))
    dscore = (probs * (dprob - delta[:, None])).astype(jnp.bfloat16)
    query_g = (jnp.einsum('rk,kd->rd', dscore.astype(jnp.float32), key_h.astype(jnp.float32)) * scale).astype(jnp.bfloat16)
    key_g = (jnp.einsum('rk,rd->kd', dscore[:, :local_count].astype(jnp.float32), query_h.astype(jnp.float32)) * scale).astype(jnp.bfloat16)
    value_g = jnp.einsum('rk,rd->kd', probs_low[:, :local_count].astype(jnp.float32), grad_h.astype(jnp.float32)).astype(jnp.bfloat16)
    return attn, query_g, key_g, value_g


def reference(queries, keys, values, track, out_weight, grad_out):
    rows = TOK_DEV
    head_dim = D // HEADS
    grad_attn = lax.dot_general(grad_out, out_weight, (((1,), (1,)), ((), ())), preferred_element_type=jnp.float32).astype(jnp.bfloat16)
    per_block = rows // BLOCK

    def split_heads(array):
        return array.reshape(array.shape[0], HEADS, head_dim).transpose(1, 0, 2)

    def one_span(span_id):
        base = span_id * rows
        q_c = lax.dynamic_slice_in_dim(queries, base, rows, 0)
        k_c = lax.dynamic_slice_in_dim(keys, base, rows, 0)
        v_c = lax.dynamic_slice_in_dim(values, base, rows, 0)
        g_c = lax.dynamic_slice_in_dim(grad_attn, base, rows, 0)
        mem_keys = []
        mem_values = []
        for distance in range(1, WINDOW + 1):
            source = jnp.maximum(span_id - distance, 0).astype(jnp.int32) * rows
            mem_keys.append(lax.dynamic_slice_in_dim(keys, source, rows, 0))
            mem_values.append(lax.dynamic_slice_in_dim(values, source, rows, 0))
        all_keys = jnp.concatenate([k_c] + mem_keys, axis=0)
        all_values = jnp.concatenate([v_c] + mem_values, axis=0)
        tracks = lax.dynamic_slice_in_dim(track, (span_id * per_block).astype(jnp.int32), per_block, 0)
        lookback = jnp.arange(WINDOW * per_block, dtype=jnp.int32) // per_block + 1
        block_ok = (tracks == 1) & (lookback[None, :] <= span_id)
        mem_ok = jnp.repeat(jnp.repeat(block_ok, BLOCK, axis=0), BLOCK, axis=1)
        position = jnp.arange(rows, dtype=jnp.int32)
        local_ok = position[:, None] >= position[None, :]
        allowed = jnp.concatenate([local_ok, mem_ok], axis=1)
        fn = jax.vmap(lambda a, b, c, d: head_grads(a, b, c, d, allowed, rows))
        attn, query_g, key_g, value_g = fn(split_heads(q_c), split_heads(all_keys), split_heads(all_values), split_heads(g_c))

        def merge_heads(array):
            return array.transpose(1, 0, 2).reshape(array.shape[1], D)

        return merge_heads(attn), merge_heads(query_g), merge_heads(key_g), merge_heads(value_g)

    attn, query_g, key_g, value_g = lax.map(one_span, jnp.arange(N_SPAN, dtype=jnp.int32))
    attn = attn.reshape(TOKENS, D)
    weight_grad = jnp.dot(attn.T, grad_out, preferred_element_type=jnp.float32)
    return query_g.reshape(TOKENS, D), key_g.reshape(TOKENS, D), value_g.reshape(TOKENS, D), weight_grad
```

```python
import functools

import jax
import jax.numpy as jnp
from jax import lax
from jax.experimental import pallas as pl
from jax.experimental.pallas import tpu as pltpu
from jax.sharding import PartitionSpec as P

HEADS = 16
BLOCK = 128
WINDOW = 8
ROW = 4
LANES = 128
NEG = -1e30
PAD = 3e30
VMEM_LIMIT = 48 * 1024 * 1024

F32 = jnp.float32
BF16 = jnp.bfloat16

ANY = pl.BlockSpec(memory_space=pl.ANY)
SMEM = pl.BlockSpec(memory_space=pltpu.SMEM)
VMEM = pl.BlockSpec(memory_space=pltpu.VMEM)


def nn(a, b):
    return lax.dot_general(a, b, (((1,), (0,)), ((), ())), preferred_element_type=F32)


def nt(a, b):
    return lax.dot_general(a, b, (((1,), (1,)), ((), ())), preferred_element_type=F32)


def params():
    return pltpu.CompilerParams(vmem_limit_bytes=VMEM_LIMIT)


def split_pair(a, b):
    lane = lax.broadcasted_iota(jnp.int32, a.shape, 1)
    low = lane < LANES // 2
    even = jnp.where(low, a, pltpu.roll(b, LANES // 2, 1))
    odd = jnp.where(low, pltpu.roll(a, LANES // 2, 1), b)
    return even, odd


def pack_kernel(me_ref, q_ref, k_ref, v_ref, t_ref, own_ref, *outs):
    first, second = outs[:ROW], outs[ROW:]
    r = me_ref[0]
    odd_me = (r % 2) == 1
    rows = q_ref.shape[0]
    per = rows // BLOCK

    def pieces(src, chunk, pair):
        tile = 4 * chunk + (r // 2 + pair) % 2
        a = src[:, pl.ds(pl.multiple_of(tile * LANES, LANES), LANES)].astype(F32)
        b = src[:, pl.ds(pl.multiple_of((tile + 2) * LANES, LANES), LANES)].astype(F32)
        even, odd = split_pair(a, b)
        return jnp.where(odd_me, odd, even), jnp.where(odd_me, even, odd)

    for chunk in (0, 1):
        for pair in (0, 1):
            for which, src in enumerate((k_ref, v_ref)):
                for side, value in enumerate(pieces(src, chunk, pair)):
                    value = value.astype(BF16)
                    d = 2 * pair + side
                    target = (first, second)[chunk][d]
                    target[which * rows : (which + 1) * rows, :] = value
                    if d == 0:
                        base = (2 * chunk + which) * rows
                        own_ref[base : base + rows, :] = value
            for side, value in enumerate(pieces(q_ref, chunk, pair)):
                d = 2 * pair + side
                scaled = value * 0.125
                for b in range(per):
                    base = 2 * rows + (chunk * per + b) * LANES
                    turned = scaled[b * BLOCK : (b + 1) * BLOCK].T
                    second[d][base : base + LANES, :] = turned.astype(BF16)
    for d in range(ROW):
        second[d][4 * rows : 4 * rows + 16, :] = t_ref[...]


def pack(me, queries, keys, values, track_block):
    rows = queries.shape[0]
    one = jax.ShapeDtypeStruct((2 * rows, LANES), BF16)
    two = jax.ShapeDtypeStruct((4 * rows + 16, LANES), BF16)
    own = jax.ShapeDtypeStruct((4 * rows, LANES), BF16)
    outs = pl.pallas_call(
        pack_kernel,
        out_shape=(own,) + (one,) * ROW + (two,) * ROW,
        in_specs=[SMEM] + [VMEM] * 4,
        out_specs=[VMEM] * 9,
        compiler_params=params(),
        name="pack",
    )(me, queries, keys, values, track_block)
    return outs[0], outs[1:5], outs[5:]


def plan_kernel(me_ref, track_ref, list_ref, count_ref):
    r = me_ref[0]
    z = me_ref[1]

    def one_query(qi, carry):
        d = qi // 2
        rho = r ^ d
        span = ROW * z + rho

        def clear(i, c):
            list_ref[qi, i] = 0
            return c

        lax.fori_loop(0, 24, clear, 0)

        def step(i, state):
            near, total = state
            u = span - (i // 2 + 1)
            use = jnp.logical_and(track_ref[qi, i] == 1, u >= 0)
            safe = jnp.maximum(u, 0)
            back = z - safe // ROW
            slot = ((back * ROW + (r ^ (safe % ROW))) * 4) + i % 2

            @pl.when(use)
            def _():
                list_ref[qi, total] = slot

            use = use.astype(jnp.int32)
            near = near + jnp.where(back < 2, use, 0)
            return near, total + use

        near, total = lax.fori_loop(0, 2 * WINDOW, step, (0, 0))
        count_ref[qi, 0] = near
        count_ref[qi, 1] = total
        return carry

    lax.fori_loop(0, 2 * ROW, one_query, 0)


def plan(me, track_row):
    return pl.pallas_call(
        plan_kernel,
        out_shape=(
            jax.ShapeDtypeStruct((2 * ROW, 24), jnp.int32),
            jax.ShapeDtypeStruct((2 * ROW, 2), jnp.int32),
        ),
        in_specs=[SMEM, SMEM],
        out_specs=[SMEM, SMEM],
        name="plan",
    )(me, track_row)


def block_diag(x):
    row = lax.broadcasted_iota(jnp.int32, x.shape, 0)
    zero = jnp.zeros_like(x)
    top = row < LANES // 2
    return jnp.concatenate([jnp.where(top, x, zero), jnp.where(top, zero, x)], axis=1)


def pick_heads(x):
    row = lax.broadcasted_iota(jnp.int32, (LANES, LANES), 0)
    return jnp.where(row < LANES // 2, x[:, :LANES], x[:, LANES:])


def causal(shape):
    key = lax.broadcasted_iota(jnp.int32, shape, 0)
    query = lax.broadcasted_iota(jnp.int32, shape, 1) % BLOCK
    return key <= query


def row_copies(chunk, rows, back, own, rest, kv, sem, slot):
    base = back * 4 * ROW
    out = []
    own_blocks = own.reshape(8, BLOCK, LANES)
    rest_blocks = rest.reshape(12, BLOCK, LANES)
    out.append(
        pltpu.make_async_copy(own_blocks.at[pl.ds(4 * chunk, 4)], kv.at[pl.ds(base, 4)], sem.at[slot])
    )
    out.append(pltpu.make_async_copy(rest_blocks, kv.at[pl.ds(base + 4, 12)], sem.at[slot + 1]))
    return out


def query_copies(chunk, seconds, qt, sem, slot):
    out = []
    for d, second in enumerate(seconds):
        blocks = second.at[pl.ds(512 + chunk * 256, 256)].reshape(2, BLOCK, LANES)
        out.append(pltpu.make_async_copy(blocks, qt.at[pl.ds(2 * d, 2)], sem.at[slot + d]))
    return out


def slots_of(list_ref, qi, start, count, how_many, base=0):
    fs, pads = [], []
    for i in range(how_many):
        position = start + i
        inside = position < count
        fs.append(jnp.where(inside, list_ref[qi, jnp.minimum(position, 23)] - base, 0))
        pads.append(jnp.where(inside, 0.0, PAD).astype(F32))
    return fs, pads


def fwd_group(kv, vt, q2, fs, pads, diag=None):
    keys = jnp.concatenate([kv[f] for f in fs], axis=0)
    scores = nn(keys, q2)
    parts = []
    top = None
    for i, pad in enumerate(pads):
        part = scores[i * BLOCK : (i + 1) * BLOCK]
        if diag == i:
            part = jnp.where(causal(part.shape), part, NEG)
        peak = jnp.maximum(jnp.max(part, axis=0, keepdims=True) - pad, NEG)
        top = peak if top is None else jnp.maximum(top, peak)
        parts.append(part)
    expo = [jnp.exp(part - (top + pad)).astype(BF16) for part, pad in zip(parts, pads)]
    turned = jnp.concatenate([vt[f] for f in fs], axis=1)
    return top, nn(turned, jnp.concatenate(expo, axis=0))


def merge(m_ref, acc_ref, qi, top, add):
    old = m_ref[qi, 0:1, :]
    new = jnp.maximum(old, top)
    acc_ref[qi] = acc_ref[qi] * jnp.exp(old - new) + add * jnp.exp(top - new)
    m_ref[qi] = jnp.broadcast_to(new, m_ref.shape[1:])


def turn_values(kv, vt, blocks, base):
    for f in blocks:
        vt[f - base, 0:LANES, :] = kv[f - base + 2].astype(F32).T.astype(BF16)
        vt[f - base, LANES : LANES + 16, :] = jnp.ones((16, LANES), BF16)


def near_kernel(
    chunk, list_ref, count_ref, own0, rest0, own1, rest1, s0, s1, s2, s3, m_ref, acc_ref, kv, vt, qt, sem
):
    copies = row_copies(chunk, 256, 0, own0, rest0, kv, sem, 0)
    copies += row_copies(chunk, 256, 1, own1, rest1, kv, sem, 2)
    copies += query_copies(chunk, (s0, s1, s2, s3), qt, sem, 4)
    for copy in copies:
        copy.start()
    for copy in copies:
        copy.wait()
    turn_values(kv, vt, [4 * i + b for i in range(2 * ROW) for b in (0, 1)], 0)
    for d in range(ROW):
        q2 = [block_diag(qt[2 * d + b]) for b in (0, 1)]
        counts = [count_ref[2 * d + b, 0] for b in (0, 1)]
        for b in (0, 1):
            qi = 2 * d + b
            fs, pads = slots_of(list_ref, qi, 0, counts[b], 2)
            fs = [4 * d, 4 * d + b] + fs
            pads = [jnp.float32(0.0 if b else PAD), jnp.float32(0.0)] + pads
            top, add = fwd_group(kv, vt, q2[b], fs, pads, diag=1)
            m_ref[qi] = jnp.broadcast_to(top, m_ref.shape[1:])
            acc_ref[qi] = add
        longest = jnp.maximum(counts[0], counts[1])

        def body(g, carry):
            for b in (0, 1):
                qi = 2 * d + b
                fs, pads = slots_of(list_ref, qi, 2 + 4 * g, counts[b], 4)
                top, add = fwd_group(kv, vt, q2[b], fs, pads)
                merge(m_ref, acc_ref, qi, top, add)
            return carry

        lax.fori_loop(0, (longest + 1) // 4, body, 0)


def near(chunk, lists, counts, own0, rest0, own1, rest1, seconds):
    return pl.pallas_call(
        functools.partial(near_kernel, chunk),
        out_shape=(
            jax.ShapeDtypeStruct((8, 8, 256), F32),
            jax.ShapeDtypeStruct((8, 144, 256), F32),
        ),
        in_specs=[SMEM, SMEM] + [ANY] * 8,
        out_specs=[VMEM, VMEM],
        scratch_shapes=[
            pltpu.VMEM((32, BLOCK, LANES), BF16),
            pltpu.VMEM((32, 144, LANES), BF16),
            pltpu.VMEM((8, LANES, BLOCK), BF16),
            pltpu.SemaphoreType.DMA((8,)),
        ],
        compiler_params=params(),
        cost_estimate=pl.CostEstimate(flops=8_000_000_000, bytes_accessed=4_000_000, transcendentals=0),
        name=f"near{chunk}",
    )(lists, counts, own0, rest0, own1, rest1, *seconds)


def far_kernel(
    chunk, fast, me_ref, list_ref, count_ref, own2, rest2, s0, s1, s2, s3, go, m_in, acc_in, *refs
):
    if fast:
        attn_ref, lse_ref, w0, w1, w2, w3, m_ref, acc_ref, kv, vt, qt, go_v, wide, sem = refs
    else:
        attn_ref, lse_ref, w0, m_ref, acc_ref, kv, vt, qt, go_v, wide, sem = refs
    copies = row_copies(chunk, 256, 0, own2, rest2, kv, sem, 0)
    copies += query_copies(chunk, (s0, s1, s2, s3), qt, sem, 2)
    copies.append(pltpu.make_async_copy(m_in, m_ref, sem.at[6]))
    copies.append(pltpu.make_async_copy(acc_in, acc_ref, sem.at[7]))
    go_copy = pltpu.make_async_copy(go, go_v, sem.at[8])
    for copy in copies:
        copy.start()
    go_copy.start()
    for copy in copies:
        copy.wait()
    base = 8 * ROW
    turn_values(kv, vt, [base + 4 * i + b for i in range(ROW) for b in (0, 1)], base)
    for d in range(ROW):
        q2 = [block_diag(qt[2 * d + b]) for b in (0, 1)]
        starts = [count_ref[2 * d + b, 0] for b in (0, 1)]
        counts = [count_ref[2 * d + b, 1] for b in (0, 1)]
        longest = jnp.maximum(counts[0] - starts[0], counts[1] - starts[1])

        def body(g, carry):
            for b in (0, 1):
                qi = 2 * d + b
                fs, pads = slots_of(list_ref, qi, starts[b] + 4 * g, counts[b], 4, base)
                top, add = fwd_group(kv, vt, q2[b], fs, pads)
                merge(m_ref, acc_ref, qi, top, add)
            return carry

        lax.fori_loop(0, (longest + 3) // 4, body, 0)
    for qi in range(2 * ROW):
        total = acc_ref[qi, LANES : LANES + 1, :]
        lse_ref[qi] = m_ref[qi] + jnp.log(jnp.broadcast_to(total, m_ref.shape[1:]))
        out = pick_heads(acc_ref[qi, 0:LANES, :] / total)
        attn_ref[:, qi * BLOCK : (qi + 1) * BLOCK] = out.astype(BF16)
    go_copy.wait()
    wide[...] = nn(attn_ref[...], go_v[...])
    if fast:
        z = me_ref[1]
        half = LANES // 2
        for delta, w in enumerate((w0, w1, w2, w3)):
            target = (z + delta) % 4 - 2 * chunk
            inside = jnp.logical_and(target >= 0, target < 2)
            at = pl.multiple_of(jnp.where(inside, target, 0) * half, half)
            piece = wide[pl.ds(at, half), :]
            w[...] = jnp.where(inside, piece, 0.0).astype(BF16)
    else:
        w0[...] = wide[...].astype(BF16)


def far(chunk, fast, me, lists, counts, own2, rest2, seconds, go, m, acc):
    width = go.shape[1]
    weights = (
        (jax.ShapeDtypeStruct((LANES // 2, width), BF16),) * 4
        if fast
        else (jax.ShapeDtypeStruct((LANES, width), BF16),)
    )
    return pl.pallas_call(
        functools.partial(far_kernel, chunk, fast),
        out_shape=(
            jax.ShapeDtypeStruct((LANES, 8 * BLOCK), BF16),
            jax.ShapeDtypeStruct((8, 8, 256), F32),
        )
        + weights,
        in_specs=[SMEM, SMEM, SMEM] + [ANY] * 9,
        out_specs=[VMEM] * (2 + len(weights)),
        scratch_shapes=[
            pltpu.VMEM((8, 8, 256), F32),
            pltpu.VMEM((8, 144, 256), F32),
            pltpu.VMEM((16, BLOCK, LANES), BF16),
            pltpu.VMEM((16, 144, LANES), BF16),
            pltpu.VMEM((8, LANES, BLOCK), BF16),
            pltpu.VMEM(go.shape, BF16),
            pltpu.VMEM((LANES, width), F32),
            pltpu.SemaphoreType.DMA((9,)),
        ],
        compiler_params=params(),
        cost_estimate=pl.CostEstimate(flops=5_000_000_000, bytes_accessed=6_000_000, transcendentals=0),
        name=f"far{chunk}",
    )(me, lists, counts, own2, rest2, *seconds, go, m, acc)


def bwd_group(kv, kt, q2, g2, lse, delta, fs, pads, diag=None):
    keys = jnp.concatenate([kv[f] for f in fs], axis=0)
    values = jnp.concatenate([kv[f + 2] for f in fs], axis=0)
    scores = nn(keys, q2)
    dprob = nn(values, g2)
    probs, dscores = [], []
    for i, pad in enumerate(pads):
        part = scores[i * BLOCK : (i + 1) * BLOCK]
        if diag == i:
            part = jnp.where(causal(part.shape), part, NEG)
        prob = jnp.exp(part - (lse + pad))
        dscore = prob * (dprob[i * BLOCK : (i + 1) * BLOCK] - delta)
        probs.append(prob)
        dscores.append(dscore.astype(BF16))
    turned = jnp.concatenate([kt[f] for f in fs], axis=1)
    return probs, dscores, nn(turned, jnp.concatenate(dscores, axis=0))


def back_kernel(
    chunk, list_ref, count_ref, own0, rest0, own1, rest1, own2, rest2, s0, s1, s2, s3,
    gt_ref, attn_ref, lse_ref, o0, o1, o2, o3, kv, kt, qt, dq, sem,
):
    copies = row_copies(chunk, 256, 0, own0, rest0, kv, sem, 0)
    copies += row_copies(chunk, 256, 1, own1, rest1, kv, sem, 2)
    copies += row_copies(chunk, 256, 2, own2, rest2, kv, sem, 4)
    copies += query_copies(chunk, (s0, s1, s2, s3), qt, sem, 6)
    for copy in copies:
        copy.start()
    for copy in copies:
        copy.wait()
    for f in [4 * i + b for i in range(3 * ROW) for b in (0, 1)]:
        kt[f] = kv[f].astype(F32).T.astype(BF16)
    outs = (o0, o1, o2, o3)
    half = LANES // 2
    for d in range(ROW):
        q2, g2, lse, delta, counts = [], [], [], [], []
        for b in (0, 1):
            qi = 2 * d + b
            gt = gt_ref[:, qi * BLOCK : (qi + 1) * BLOCK]
            product = gt.astype(F32) * attn_ref[:, qi * BLOCK : (qi + 1) * BLOCK].astype(F32)
            delta.append(
                jnp.concatenate(
                    [
                        jnp.sum(product[:half], axis=0, keepdims=True),
                        jnp.sum(product[half:], axis=0, keepdims=True),
                    ],
                    axis=1,
                )
            )
            q2.append(block_diag(qt[qi]))
            g2.append(block_diag(gt))
            lse.append(lse_ref[qi, 0:1, :])
            counts.append(count_ref[qi, 1])
        local = []
        for b in (0, 1):
            qi = 2 * d + b
            fs, pads = slots_of(list_ref, qi, 0, counts[b], 2)
            fs = [4 * d, 4 * d + b] + fs
            pads = [jnp.float32(0.0 if b else PAD), jnp.float32(0.0)] + pads
            probs, dscores, add = bwd_group(
                kv, kt, q2[b], g2[b], lse[b], delta[b], fs, pads, diag=1
            )
            dq[b] = add
            local.append(([p.astype(BF16) for p in probs[:2]], dscores[:2]))
        q_both = jnp.concatenate(q2, axis=1)
        g_both = jnp.concatenate(g2, axis=1)
        out = outs[d]
        out[256:384, :] = nt(
            jnp.concatenate([local[0][1][1], local[1][1][0]], axis=1), q_both
        ).astype(BF16)
        out[384:512, :] = nt(local[1][1][1], q2[1]).astype(BF16)
        out[512:640, :] = nt(
            jnp.concatenate([local[0][0][1], local[1][0][0]], axis=1), g_both
        ).astype(BF16)
        out[640:768, :] = nt(local[1][0][1], g2[1]).astype(BF16)
        longest = jnp.maximum(counts[0], counts[1])

        def body(g, carry):
            for b in (0, 1):
                qi = 2 * d + b
                fs, pads = slots_of(list_ref, qi, 2 + 4 * g, counts[b], 4)
                _, _, add = bwd_group(kv, kt, q2[b], g2[b], lse[b], delta[b], fs, pads)
                dq[b] += add
            return carry

        lax.fori_loop(0, (longest + 1) // 4, body, 0)
        for b in (0, 1):
            grad = pick_heads(dq[b]) * 0.125
            out[b * BLOCK : (b + 1) * BLOCK, :] = grad.T.astype(BF16)


def back(chunk, lists, counts, row0, row1, row2, seconds, gt, attn, lse):
    return pl.pallas_call(
        functools.partial(back_kernel, chunk),
        out_shape=(jax.ShapeDtypeStruct((768, LANES), BF16),) * 4,
        in_specs=[SMEM, SMEM] + [ANY] * 10 + [VMEM] * 3,
        out_specs=[VMEM] * 4,
        scratch_shapes=[
            pltpu.VMEM((48, BLOCK, LANES), BF16),
            pltpu.VMEM((48, LANES, BLOCK), BF16),
            pltpu.VMEM((8, LANES, BLOCK), BF16),
            pltpu.VMEM((2, LANES, 256), F32),
            pltpu.SemaphoreType.DMA((10,)),
        ],
        compiler_params=params(),
        cost_estimate=pl.CostEstimate(flops=10_000_000_000, bytes_accessed=8_000_000, transcendentals=0),
        name=f"back{chunk}",
    )(lists, counts, *row0, *row1, *row2, *seconds, gt, attn, lse)


def unpack_kernel(me_ref, *refs):
    ins, outs = refs[:8], refs[8:]
    r = me_ref[0]
    odd_me = (r % 2) == 1
    rows = outs[0].shape[0]
    for chunk in (0, 1):
        for pair in (0, 1):
            tile = 4 * chunk + (r // 2 + pair) % 2
            first, second = ins[4 * chunk + 2 * pair], ins[4 * chunk + 2 * pair + 1]
            for which, out in enumerate(outs):
                a = first[which * rows : (which + 1) * rows, :].astype(F32)
                b = second[which * rows : (which + 1) * rows, :].astype(F32)
                low, high = jnp.where(odd_me, b, a), jnp.where(odd_me, a, b)
                one, two = split_pair(low, high)
                at = pl.multiple_of(tile * LANES, LANES)
                out[:, pl.ds(at, LANES)] = one.astype(BF16)
                at = pl.multiple_of((tile + 2) * LANES, LANES)
                out[:, pl.ds(at, LANES)] = two.astype(BF16)


def unpack(me, pieces, rows, width):
    return pl.pallas_call(
        unpack_kernel,
        out_shape=(jax.ShapeDtypeStruct((rows, width), BF16),) * 3,
        in_specs=[SMEM] + [VMEM] * 8,
        out_specs=[VMEM] * 3,
        compiler_params=params(),
        name="unpack",
    )(me, *pieces)


def swap(value, axis, bit):
    count = lax.axis_size(axis)
    return lax.ppermute(value, axis, [(s, s ^ bit) for s in range(count)])


def later(value, axis):
    count = lax.axis_size(axis)
    return lax.ppermute(value, axis, [(s, s + ROW) for s in range(count - ROW)])


def shards(queries, keys, values, track, out_weight, grad_out):
    rows, width = queries.shape
    count = lax.axis_size("span")
    index = lax.axis_index("span").astype(jnp.int32)
    r, z = index % ROW, index // ROW
    me = jnp.stack([r, z])
    fast = count == HEADS
    track_block = jnp.pad(track.astype(BF16), ((0, 14), (0, LANES - track.shape[1])))
    own0, firsts, seconds = pack(me, queries, keys, values, track_block)

    own1 = later(own0, "span")
    got_first = [swap(firsts[d], "span", d) for d in (1, 2, 3)]
    got_second = [swap(seconds[d], "span", d) for d in (1, 2, 3)]
    own2 = later(own1, "span")
    seconds = [seconds[0]] + got_second
    rest0 = [
        jnp.concatenate(got_first, axis=0),
        jnp.concatenate([x[: 2 * rows] for x in got_second], axis=0),
    ]
    rest1 = [later(x, "span") for x in rest0]
    rest2 = [later(x, "span") for x in rest1]

    go2 = swap(grad_out, "span", 2)
    go1 = swap(grad_out, "span", 1)
    go3 = swap(go2, "span", 1)
    go = jnp.concatenate([grad_out, go1, go2, go3], axis=0)

    track_row = jnp.concatenate([x[4 * rows : 4 * rows + 2, : 2 * WINDOW] for x in seconds], axis=0)
    lists, counts = plan(me, track_row.astype(jnp.int32))

    head_dim = width // HEADS
    weight_rows = lax.dynamic_index_in_dim(
        out_weight.reshape(ROW, ROW, head_dim, width), r, 1, keepdims=False
    ).reshape(ROW * head_dim, width)
    grad_turned = lax.dot_general(
        weight_rows, go, (((1,), (1,)), ((), ())), preferred_element_type=F32
    ).astype(BF16)

    states, pieces, weights = [], [], []
    for chunk in (0, 1):
        states.append(near(chunk, lists, counts, own0, rest0[chunk], own1, rest1[chunk], seconds))
    for chunk in (0, 1):
        attn, lse, *terms = far(
            chunk, fast, me, lists, counts, own2, rest2[chunk], seconds, go, *states[chunk]
        )
        if fast:
            received = [terms[0].astype(F32)]
            for delta in (1, 2, 3):
                pairs = [
                    (ROW * s + q, ROW * ((s + delta) % ROW) + q)
                    for s in range(ROW)
                    for q in range(ROW)
                    if (s + delta) % ROW // 2 == chunk
                ]
                received.append(lax.ppermute(terms[delta], "span", pairs).astype(F32))
            weights += received
        else:
            weights.append(terms[0])
        out = back(
            chunk,
            lists,
            counts,
            (own0, rest0[chunk]),
            (own1, rest1[chunk]),
            (own2, rest2[chunk]),
            seconds,
            grad_turned[chunk * LANES : (chunk + 1) * LANES],
            attn,
            lse,
        )
        pieces.append(out[0])
        pieces += [swap(out[d], "span", d) for d in (1, 2, 3)]
    query_grad, key_grad, value_grad = unpack(me, pieces, rows, width)
    if fast:
        weight_grad = functools.reduce(lambda a, b: a + b, weights)
    else:
        mine = jnp.concatenate(weights, axis=0).reshape(ROW, 1, head_dim, width)
        full = jnp.zeros((ROW, ROW, head_dim, width), BF16)
        full = lax.dynamic_update_slice(full, mine, (0, r, 0, 0)).reshape(width, width)
        weight_grad = lax.psum_scatter(full.astype(F32), "span", scatter_dimension=0, tiled=True)
    return (query_grad, key_grad, value_grad, weight_grad)


def solution(mesh):
    spec = P(("groups", "span"), None)
    return jax.shard_map(
        shards,
        mesh=mesh,
        in_specs=(spec, spec, spec, spec, P(), spec),
        out_specs=(spec, spec, spec, spec),
        check_vma=False,
    )
```

```python
import functools

import jax
import jax.numpy as jnp
from jax import lax
from jax.experimental import pallas as pl
from jax.experimental.pallas import tpu as pltpu
from jax.sharding import PartitionSpec as P

HEADS = 16
BLOCK = 128
WINDOW = 8
ROW = 4
LANES = 128
NEG = -1e30
PAD = 3e30
VMEM_LIMIT = 16 * 1024 * 1024
SMALL = pl.CostEstimate(flops=1_000_000, bytes_accessed=100_000, transcendentals=0)

F32 = jnp.float32
BF16 = jnp.bfloat16

ANY = pl.BlockSpec(memory_space=pl.ANY)
SMEM = pl.BlockSpec(memory_space=pltpu.SMEM)
VMEM = pl.BlockSpec(memory_space=pltpu.VMEM)


def nn(a, b):
    return lax.dot_general(a, b, (((1,), (0,)), ((), ())), preferred_element_type=F32)


def nt(a, b):
    return lax.dot_general(a, b, (((1,), (1,)), ((), ())), preferred_element_type=F32)


def params():
    return pltpu.CompilerParams(vmem_limit_bytes=VMEM_LIMIT)


def split_pair(a, b):
    lane = lax.broadcasted_iota(jnp.int32, a.shape, 1)
    low = lane < LANES // 2
    even = jnp.where(low, a, pltpu.roll(b, LANES // 2, 1))
    odd = jnp.where(low, pltpu.roll(a, LANES // 2, 1), b)
    return even, odd


def packed(me_ref, src, chunk, pair):
    r = me_ref[0]
    odd_me = (r % 2) == 1
    tile = 4 * chunk + (r // 2 + pair) % 2
    a = src[:, pl.ds(pl.multiple_of(tile * LANES, LANES), LANES)].astype(F32)
    b = src[:, pl.ds(pl.multiple_of((tile + 2) * LANES, LANES), LANES)].astype(F32)
    even, odd = split_pair(a, b)
    return jnp.where(odd_me, odd, even), jnp.where(odd_me, even, odd)


def pack_first_kernel(me_ref, k_ref, v_ref, own_ref, *outs):
    rows = k_ref.shape[0]
    for which, src in enumerate((k_ref, v_ref)):
        for side, value in enumerate(packed(me_ref, src, 1, 0)):
            if side == 0:
                base = (2 + which) * rows
                own_ref[base : base + rows, :] = value.astype(BF16)
        for pair in (0, 1):
            for side, value in enumerate(packed(me_ref, src, 0, pair)):
                d = 2 * pair + side
                value = value.astype(BF16)
                base = which * rows
                if d == 0:
                    own_ref[base : base + rows, :] = value
                else:
                    outs[d - 1][base : base + rows, :] = value


def pack_second_kernel(me_ref, q_ref, k_ref, v_ref, t_ref, *outs):
    rows = k_ref.shape[0]
    per = rows // BLOCK
    for pair in (0, 1):
        for which, src in enumerate((k_ref, v_ref)):
            for side, value in enumerate(packed(me_ref, src, 1, pair)):
                outs[2 * pair + side][which * rows : (which + 1) * rows, :] = value.astype(BF16)
        for chunk in (0, 1):
            for side, value in enumerate(packed(me_ref, q_ref, chunk, pair)):
                scaled = value * 0.125
                for b in range(per):
                    base = 2 * rows + (chunk * per + b) * LANES
                    turned = scaled[b * BLOCK : (b + 1) * BLOCK].T
                    outs[2 * pair + side][base : base + LANES, :] = turned.astype(BF16)
    for out in outs:
        out[4 * rows : 4 * rows + 16, :] = t_ref[...]


def pack_first(me, keys, values):
    rows = keys.shape[0]
    outs = pl.pallas_call(
        pack_first_kernel,
        out_shape=(jax.ShapeDtypeStruct((4 * rows, LANES), BF16),)
        + (jax.ShapeDtypeStruct((2 * rows, LANES), BF16),) * 3,
        in_specs=[SMEM] + [VMEM] * 2,
        out_specs=[VMEM] * 4,
        compiler_params=params(),
        cost_estimate=SMALL,
        name="pack_first",
    )(me, keys, values)
    return outs[0], outs[1:]


def pack_second(me, queries, keys, values, track_block):
    rows = queries.shape[0]
    return pl.pallas_call(
        pack_second_kernel,
        out_shape=(jax.ShapeDtypeStruct((4 * rows + 16, LANES), BF16),) * ROW,
        in_specs=[SMEM] + [VMEM] * 4,
        out_specs=[VMEM] * ROW,
        compiler_params=params(),
        cost_estimate=SMALL,
        name="pack_second",
    )(me, queries, keys, values, track_block)


def stack_kernel(rows, a, b, c, out):
    for i, src in enumerate((a, b, c)):
        out[i * rows : (i + 1) * rows, :] = src[0:rows, :]


def stack(rows, pieces):
    return pl.pallas_call(
        functools.partial(stack_kernel, rows),
        out_shape=jax.ShapeDtypeStruct((3 * rows, LANES), BF16),
        in_specs=[VMEM] * 3,
        out_specs=VMEM,
        compiler_params=params(),
        cost_estimate=SMALL,
        name="stack",
    )(*pieces)


def grad_kernel(me_ref, w, g0, g1, g2, g3, out, wide_w, wide_g, sem):
    r = me_ref[0]
    half = LANES // 2
    rows = g0.shape[0]
    copies = [
        pltpu.make_async_copy(
            w.at[pl.ds(pl.multiple_of((ROW * j + r) * half, half), half)],
            wide_w.at[pl.ds(j * half, half)],
            sem.at[j],
        )
        for j in range(ROW)
    ]
    copies += [
        pltpu.make_async_copy(g, wide_g.at[pl.ds(d * rows, rows)], sem.at[ROW + d])
        for d, g in enumerate((g0, g1, g2, g3))
    ]
    for copy in copies:
        copy.start()
    for copy in copies:
        copy.wait()
    for d in range(ROW):
        piece = wide_g[d * rows : (d + 1) * rows, :]
        out[:, d * rows : (d + 1) * rows] = nt(wide_w[...], piece).astype(BF16)


def grad_turned(me, weight, gos):
    rows, width = gos[0].shape
    return pl.pallas_call(
        grad_kernel,
        out_shape=jax.ShapeDtypeStruct((2 * LANES, ROW * rows), BF16),
        in_specs=[SMEM] + [ANY] * 5,
        out_specs=VMEM,
        scratch_shapes=[
            pltpu.VMEM((2 * LANES, width), BF16),
            pltpu.VMEM((ROW * rows, width), BF16),
            pltpu.SemaphoreType.DMA((2 * ROW,)),
        ],
        compiler_params=params(),
        cost_estimate=SMALL,
        name="grad_attn",
    )(me, weight, *gos)


def plan_kernel(me_ref, track_ref, list_ref, count_ref):
    r = me_ref[0]
    z = me_ref[1]

    def one_query(qi, carry):
        d = qi // 2
        rho = r ^ d
        span = ROW * z + rho

        near, total = jnp.int32(0), jnp.int32(0)
        for i in range(2 * WINDOW):
            u = span - (i // 2 + 1)
            use = jnp.logical_and(track_ref[qi, i] == 1, u >= 0).astype(jnp.int32)
            safe = jnp.maximum(u, 0)
            back = z - safe // ROW
            list_ref[qi, total] = ((back * ROW + (r ^ (safe % ROW))) * 4) + i % 2
            near = near + jnp.where(back < 2, use, 0)
            total = total + use
        count_ref[qi, 0] = near
        count_ref[qi, 1] = total
        return carry

    lax.fori_loop(0, 2 * ROW, one_query, 0)


def plan(me, track_row):
    return pl.pallas_call(
        plan_kernel,
        out_shape=(
            jax.ShapeDtypeStruct((2 * ROW, 24), jnp.int32),
            jax.ShapeDtypeStruct((2 * ROW, 2), jnp.int32),
        ),
        in_specs=[SMEM, SMEM],
        out_specs=[SMEM, SMEM],
        cost_estimate=SMALL,
        name="plan",
    )(me, track_row)


def block_diag(x):
    row = lax.broadcasted_iota(jnp.int32, x.shape, 0)
    zero = jnp.zeros_like(x)
    top = row < LANES // 2
    return jnp.concatenate([jnp.where(top, x, zero), jnp.where(top, zero, x)], axis=1)


def pick_heads(x):
    row = lax.broadcasted_iota(jnp.int32, (LANES, LANES), 0)
    return jnp.where(row < LANES // 2, x[:, :LANES], x[:, LANES:])


def causal(shape):
    key = lax.broadcasted_iota(jnp.int32, shape, 0)
    query = lax.broadcasted_iota(jnp.int32, shape, 1) % BLOCK
    return key <= query


def row_copies(chunk, rows, back, own, rest, kv, sem, slot):
    base = back * 4 * ROW
    out = []
    own_blocks = own.reshape(8, BLOCK, LANES)
    rest_blocks = rest.reshape(12, BLOCK, LANES)
    out.append(
        pltpu.make_async_copy(own_blocks.at[pl.ds(4 * chunk, 4)], kv.at[pl.ds(base, 4)], sem.at[slot])
    )
    out.append(pltpu.make_async_copy(rest_blocks, kv.at[pl.ds(base + 4, 12)], sem.at[slot + 1]))
    return out


def query_copies(chunk, seconds, qt, sem, slot):
    out = []
    for d, second in enumerate(seconds):
        blocks = second.at[pl.ds(512 + chunk * 256, 256)].reshape(2, BLOCK, LANES)
        out.append(pltpu.make_async_copy(blocks, qt.at[pl.ds(2 * d, 2)], sem.at[slot + d]))
    return out


def slots_of(list_ref, qi, start, count, how_many, base=0):
    fs, pads = [], []
    for i in range(how_many):
        position = start + i
        inside = position < count
        fs.append(jnp.where(inside, list_ref[qi, jnp.minimum(position, 23)] - base, 0))
        pads.append(jnp.where(inside, 0.0, PAD).astype(F32))
    return fs, pads


def fwd_group(kv, vt, q2, fs, pads, diag=None):
    keys = jnp.concatenate([kv[f] for f in fs], axis=0)
    scores = nn(keys, q2)
    parts = []
    top = None
    for i, pad in enumerate(pads):
        part = scores[i * BLOCK : (i + 1) * BLOCK]
        if diag == i:
            part = jnp.where(causal(part.shape), part, NEG)
        peak = jnp.maximum(jnp.max(part, axis=0, keepdims=True) - pad, NEG)
        top = peak if top is None else jnp.maximum(top, peak)
        parts.append(part)
    expo = [jnp.exp(part - (top + pad)).astype(BF16) for part, pad in zip(parts, pads)]
    turned = jnp.concatenate([vt[f] for f in fs], axis=1)
    return top, nn(turned, jnp.concatenate(expo, axis=0))


def merge(m_ref, acc_ref, qi, top, add):
    old = m_ref[qi, 0:1, :]
    new = jnp.maximum(old, top)
    acc_ref[qi] = acc_ref[qi] * jnp.exp(old - new) + add * jnp.exp(top - new)
    m_ref[qi] = jnp.broadcast_to(new, m_ref.shape[1:])


def turn_values(kv, vt, blocks, base):
    for f in blocks:
        vt[f - base, 0:LANES, :] = kv[f - base + 2].astype(F32).T.astype(BF16)
        vt[f - base, LANES : LANES + 16, :] = jnp.ones((16, LANES), BF16)


def near_kernel(
    chunk, list_ref, count_ref, own0, rest0, own1, rest1, s0, s1, s2, s3, after, m_ref, acc_ref, kv, vt, qt, sem
):
    copies = row_copies(chunk, 256, 0, own0, rest0, kv, sem, 0)
    copies += row_copies(chunk, 256, 1, own1, rest1, kv, sem, 2)
    copies += query_copies(chunk, (s0, s1, s2, s3), qt, sem, 4)
    for copy in copies:
        copy.start()
    for copy in copies:
        copy.wait()
    turn_values(kv, vt, [4 * i + b for i in range(2 * ROW) for b in (0, 1)], 0)
    for d in range(ROW):
        q2 = [block_diag(qt[2 * d + b]) for b in (0, 1)]
        counts = [count_ref[2 * d + b, 0] for b in (0, 1)]
        for b in (0, 1):
            qi = 2 * d + b
            fs, pads = slots_of(list_ref, qi, 0, counts[b], 2)
            fs = [4 * d, 4 * d + b] + fs
            pads = [jnp.float32(0.0 if b else PAD), jnp.float32(0.0)] + pads
            top, add = fwd_group(kv, vt, q2[b], fs, pads, diag=1)
            m_ref[qi] = jnp.broadcast_to(top, m_ref.shape[1:])
            acc_ref[qi] = add
        longest = jnp.maximum(counts[0], counts[1])

        def body(g, carry):
            for b in (0, 1):
                qi = 2 * d + b
                fs, pads = slots_of(list_ref, qi, 2 + 4 * g, counts[b], 4)
                top, add = fwd_group(kv, vt, q2[b], fs, pads)
                merge(m_ref, acc_ref, qi, top, add)
            return carry

        lax.fori_loop(0, (longest + 1) // 4, body, 0)


def near(chunk, lists, counts, own0, rest0, own1, rest1, seconds, after):
    return pl.pallas_call(
        functools.partial(near_kernel, chunk),
        out_shape=(
            jax.ShapeDtypeStruct((8, 8, 256), F32),
            jax.ShapeDtypeStruct((8, 144, 256), F32),
        ),
        in_specs=[SMEM, SMEM] + [ANY] * 9,
        out_specs=[VMEM, VMEM],
        scratch_shapes=[
            pltpu.VMEM((32, BLOCK, LANES), BF16),
            pltpu.VMEM((32, 144, LANES), BF16),
            pltpu.VMEM((8, LANES, BLOCK), BF16),
            pltpu.SemaphoreType.DMA((8,)),
        ],
        compiler_params=params(),
        cost_estimate=SMALL,
        name=f"near{chunk}",
    )(lists, counts, own0, rest0, own1, rest1, *seconds, after)


def far_kernel(
    chunk, last, me_ref, list_ref, count_ref, own2, rest2, s0, s1, s2, s3, g0, g1, g2, g3,
    m_in, acc_in, after, earlier, attn_ref, lse_ref, *refs
):
    *terms, m_ref, acc_ref, kv, vt, qt, go_v, wide, sem = refs
    copies = row_copies(chunk, 256, 0, own2, rest2, kv, sem, 0)
    copies += query_copies(chunk, (s0, s1, s2, s3), qt, sem, 2)
    copies.append(pltpu.make_async_copy(m_in, m_ref, sem.at[6]))
    copies.append(pltpu.make_async_copy(acc_in, acc_ref, sem.at[7]))
    late = [
        pltpu.make_async_copy(g, go_v.at[pl.ds(d * 256, 256)], sem.at[8 + d])
        for d, g in enumerate((g0, g1, g2, g3))
    ]
    if last:
        late.append(pltpu.make_async_copy(earlier, wide.at[pl.ds(0, LANES)], sem.at[12]))
    for copy in copies:
        copy.start()
    for copy in late:
        copy.start()
    for copy in copies:
        copy.wait()
    base = 8 * ROW
    turn_values(kv, vt, [base + 4 * i + b for i in range(ROW) for b in (0, 1)], base)
    for d in range(ROW):
        q2 = [block_diag(qt[2 * d + b]) for b in (0, 1)]
        starts = [count_ref[2 * d + b, 0] for b in (0, 1)]
        counts = [count_ref[2 * d + b, 1] for b in (0, 1)]
        longest = jnp.maximum(counts[0] - starts[0], counts[1] - starts[1])

        def body(g, carry):
            for b in (0, 1):
                qi = 2 * d + b
                fs, pads = slots_of(list_ref, qi, starts[b] + 4 * g, counts[b], 4, base)
                top, add = fwd_group(kv, vt, q2[b], fs, pads)
                merge(m_ref, acc_ref, qi, top, add)
            return carry

        lax.fori_loop(0, (longest + 3) // 4, body, 0)
    for qi in range(2 * ROW):
        total = acc_ref[qi, LANES : LANES + 1, :]
        lse_ref[qi] = m_ref[qi] + jnp.log(jnp.broadcast_to(total, m_ref.shape[1:]))
        out = pick_heads(acc_ref[qi, 0:LANES, :] / total)
        attn_ref[:, qi * BLOCK : (qi + 1) * BLOCK] = out.astype(BF16)
    for copy in late:
        copy.wait()
    term = nn(attn_ref[...], go_v[...])
    if not last:
        terms[0][...] = term.astype(BF16)
        return
    wide[LANES : 2 * LANES, :] = term.astype(BF16)
    z = me_ref[1]
    half = LANES // 2
    for delta, out in enumerate(terms):
        at = pl.multiple_of((z + delta) % ROW * half, half)
        out[...] = wide[pl.ds(at, half), :]


def far(chunk, last, me, lists, counts, own2, rest2, seconds, gos, m, acc, after, earlier):
    width = gos[0].shape[1]
    weights = (
        (jax.ShapeDtypeStruct((LANES // 2, width), BF16),) * 4
        if last
        else (jax.ShapeDtypeStruct((LANES, width), BF16),)
    )
    return pl.pallas_call(
        functools.partial(far_kernel, chunk, last),
        out_shape=(
            jax.ShapeDtypeStruct((LANES, 8 * BLOCK), BF16),
            jax.ShapeDtypeStruct((8, 8, 256), F32),
        )
        + weights,
        in_specs=[SMEM, SMEM, SMEM] + [ANY] * 14,
        out_specs=[VMEM] * (2 + len(weights)),
        scratch_shapes=[
            pltpu.VMEM((8, 8, 256), F32),
            pltpu.VMEM((8, 144, 256), F32),
            pltpu.VMEM((16, BLOCK, LANES), BF16),
            pltpu.VMEM((16, 144, LANES), BF16),
            pltpu.VMEM((8, LANES, BLOCK), BF16),
            pltpu.VMEM((ROW * gos[0].shape[0], width), BF16),
            pltpu.VMEM((2 * LANES, width), BF16),
            pltpu.SemaphoreType.DMA((13,)),
        ],
        compiler_params=params(),
        cost_estimate=SMALL,
        name=f"far{chunk}",
    )(me, lists, counts, own2, rest2, *seconds, *gos, m, acc, after, earlier)


def bwd_group(kv, kt, q2, g2, lse, delta, fs, pads, diag=None):
    keys = jnp.concatenate([kv[f] for f in fs], axis=0)
    values = jnp.concatenate([kv[f + 2] for f in fs], axis=0)
    scores = nn(keys, q2)
    dprob = nn(values, g2)
    probs, dscores = [], []
    for i, pad in enumerate(pads):
        part = scores[i * BLOCK : (i + 1) * BLOCK]
        if diag == i:
            part = jnp.where(causal(part.shape), part, NEG)
        prob = jnp.exp(part - (lse + pad))
        dscore = prob * (dprob[i * BLOCK : (i + 1) * BLOCK] - delta)
        probs.append(prob)
        dscores.append(dscore.astype(BF16))
    turned = jnp.concatenate([kt[f] for f in fs], axis=1)
    return probs, dscores, nn(turned, jnp.concatenate(dscores, axis=0))


def back_kernel(
    chunk, list_ref, count_ref, own0, rest0, own1, rest1, own2, rest2, s0, s1, s2, s3,
    gt_ref, attn_ref, lse_ref, o0, o1, o2, o3, kv, kt, qt, dq, sem,
):
    copies = row_copies(chunk, 256, 0, own0, rest0, kv, sem, 0)
    copies += row_copies(chunk, 256, 1, own1, rest1, kv, sem, 2)
    copies += row_copies(chunk, 256, 2, own2, rest2, kv, sem, 4)
    copies += query_copies(chunk, (s0, s1, s2, s3), qt, sem, 6)
    for copy in copies:
        copy.start()
    for copy in copies:
        copy.wait()
    for f in [4 * i + b for i in range(3 * ROW) for b in (0, 1)]:
        kt[f] = kv[f].astype(F32).T.astype(BF16)
    outs = (o0, o1, o2, o3)
    half = LANES // 2
    for d in range(ROW):
        q2, g2, lse, delta, counts = [], [], [], [], []
        for b in (0, 1):
            qi = 2 * d + b
            gt = gt_ref[:, qi * BLOCK : (qi + 1) * BLOCK]
            product = gt.astype(F32) * attn_ref[:, qi * BLOCK : (qi + 1) * BLOCK].astype(F32)
            delta.append(
                jnp.concatenate(
                    [
                        jnp.sum(product[:half], axis=0, keepdims=True),
                        jnp.sum(product[half:], axis=0, keepdims=True),
                    ],
                    axis=1,
                )
            )
            q2.append(block_diag(qt[qi]))
            g2.append(block_diag(gt))
            lse.append(lse_ref[qi, 0:1, :])
            counts.append(count_ref[qi, 1])
        local = []
        for b in (0, 1):
            qi = 2 * d + b
            fs, pads = slots_of(list_ref, qi, 0, counts[b], 2)
            fs = [4 * d, 4 * d + b] + fs
            pads = [jnp.float32(0.0 if b else PAD), jnp.float32(0.0)] + pads
            probs, dscores, add = bwd_group(
                kv, kt, q2[b], g2[b], lse[b], delta[b], fs, pads, diag=1
            )
            dq[b] = add
            local.append(([p.astype(BF16) for p in probs[:2]], dscores[:2]))
        q_both = jnp.concatenate(q2, axis=1)
        g_both = jnp.concatenate(g2, axis=1)
        out = outs[d]
        out[256:384, :] = nt(
            jnp.concatenate([local[0][1][1], local[1][1][0]], axis=1), q_both
        ).astype(BF16)
        out[384:512, :] = nt(local[1][1][1], q2[1]).astype(BF16)
        out[512:640, :] = nt(
            jnp.concatenate([local[0][0][1], local[1][0][0]], axis=1), g_both
        ).astype(BF16)
        out[640:768, :] = nt(local[1][0][1], g2[1]).astype(BF16)
        longest = jnp.maximum(counts[0], counts[1])

        def body(g, carry):
            for b in (0, 1):
                qi = 2 * d + b
                fs, pads = slots_of(list_ref, qi, 2 + 4 * g, counts[b], 4)
                _, _, add = bwd_group(kv, kt, q2[b], g2[b], lse[b], delta[b], fs, pads)
                dq[b] += add
            return carry

        lax.fori_loop(0, (longest + 1) // 4, body, 0)
        for b in (0, 1):
            grad = pick_heads(dq[b]) * 0.125
            out[b * BLOCK : (b + 1) * BLOCK, :] = grad.T.astype(BF16)


def back(chunk, lists, counts, row0, row1, row2, seconds, gt, attn, lse):
    return pl.pallas_call(
        functools.partial(back_kernel, chunk),
        out_shape=(jax.ShapeDtypeStruct((768, LANES), BF16),) * 4,
        in_specs=[SMEM, SMEM] + [ANY] * 10 + [VMEM] * 3,
        out_specs=[VMEM] * 4,
        scratch_shapes=[
            pltpu.VMEM((48, BLOCK, LANES), BF16),
            pltpu.VMEM((48, LANES, BLOCK), BF16),
            pltpu.VMEM((8, LANES, BLOCK), BF16),
            pltpu.VMEM((2, LANES, 256), F32),
            pltpu.SemaphoreType.DMA((10,)),
        ],
        compiler_params=params(),
        cost_estimate=SMALL,
        name=f"back{chunk}",
    )(lists, counts, *row0, *row1, *row2, *seconds, gt, attn, lse)


def unpack_kernel(me_ref, *refs):
    ins, outs = refs[:8], refs[8:]
    r = me_ref[0]
    odd_me = (r % 2) == 1
    rows = outs[0].shape[0]
    for chunk in (0, 1):
        for pair in (0, 1):
            tile = 4 * chunk + (r // 2 + pair) % 2
            first, second = ins[4 * chunk + 2 * pair], ins[4 * chunk + 2 * pair + 1]
            for which, out in enumerate(outs):
                a = first[which * rows : (which + 1) * rows, :].astype(F32)
                b = second[which * rows : (which + 1) * rows, :].astype(F32)
                low, high = jnp.where(odd_me, b, a), jnp.where(odd_me, a, b)
                one, two = split_pair(low, high)
                at = pl.multiple_of(tile * LANES, LANES)
                out[:, pl.ds(at, LANES)] = one.astype(BF16)
                at = pl.multiple_of((tile + 2) * LANES, LANES)
                out[:, pl.ds(at, LANES)] = two.astype(BF16)


def unpack(me, pieces, rows, width):
    return pl.pallas_call(
        unpack_kernel,
        out_shape=(jax.ShapeDtypeStruct((rows, width), BF16),) * 3,
        in_specs=[SMEM] + [VMEM] * 8,
        out_specs=[VMEM] * 3,
        compiler_params=params(),
        cost_estimate=SMALL,
        name="unpack",
    )(me, *pieces)


def swap(value, axis, bit):
    count = lax.axis_size(axis)
    return lax.ppermute(value, axis, [(s, s ^ bit) for s in range(count)])


def later(value, axis):
    count = lax.axis_size(axis)
    return lax.ppermute(value, axis, [(s, s + ROW) for s in range(count - ROW)])


hold = lax.optimization_barrier


def shards(queries, keys, values, track, out_weight, grad_out):
    rows, width = queries.shape
    count = lax.axis_size("span")
    index = lax.axis_index("span").astype(jnp.int32)
    r, z = index % ROW, index // ROW
    me = jnp.stack([r, z])
    fast = count == HEADS
    track_block = jnp.pad(track.astype(BF16), ((0, 14), (0, LANES - track.shape[1])))

    own0, firsts = pack_first(me, keys, values)
    own1 = later(own0, "span")
    got_first = [swap(x, "span", d + 1) for d, x in enumerate(firsts)]
    rest0 = [stack(2 * rows, got_first)]
    rest1 = [later(rest0[0], "span")]

    queries, _ = hold((queries, got_first[0]))
    seconds = list(pack_second(me, queries, keys, values, track_block))
    seconds, _ = hold((seconds, (rest0[0], own1)))
    seconds[1:] = [swap(seconds[d], "span", d) for d in (1, 2, 3)]
    own2 = later(own1, "span")
    track_row = jnp.concatenate([x[4 * rows : 4 * rows + 2, : 2 * WINDOW] for x in seconds], axis=0)
    lists, counts = plan(me, track_row.astype(jnp.int32))
    arrived, _ = hold((seconds[1:], (rest1[0], own2, lists)))
    rest0.append(stack(2 * rows, arrived))
    rest1.append(later(rest0[1], "span"))
    rest2 = [later(x, "span") for x in rest1]
    grad_late, _ = hold((grad_out, rest0[1]))
    go2 = swap(grad_late, "span", 2)

    states, pieces = [], []
    after = lists
    for chunk in (0, 1):
        states.append(near(chunk, lists, counts, own0, rest0[chunk], own1, rest1[chunk], seconds, after))
        after = states[-1][0]
        if chunk == 0:
            (grad_late, go2), _ = hold(((grad_out, go2), after))
            gos = (grad_out, swap(grad_late, "span", 1), go2, swap(go2, "span", 1))
            grads = grad_turned(me, out_weight, gos)
    terms = [after]
    for chunk in (0, 1):
        last = chunk == 1 and fast
        attn, lse, *terms = far(
            chunk, last, me, lists, counts, own2, rest2[chunk], seconds, gos, *states[chunk],
            after, terms[0],
        )
        if last:
            weight_grad = terms[0].astype(F32)
            for delta in (1, 2, 3):
                pairs = [
                    (ROW * s + q, ROW * ((s + delta) % ROW) + q)
                    for s in range(ROW)
                    for q in range(ROW)
                ]
                weight_grad += lax.ppermute(terms[delta], "span", pairs).astype(F32)
        elif not fast:
            pieces_w = [terms[0]] if chunk == 0 else [pieces_w[0], terms[0]]
        out = back(
            chunk,
            lists,
            counts,
            (own0, rest0[chunk]),
            (own1, rest1[chunk]),
            (own2, rest2[chunk]),
            seconds,
            grads[chunk * LANES : (chunk + 1) * LANES],
            attn,
            lse,
        )
        after = out[0]
        if chunk == 1:
            out, pieces = hold((out, pieces))
        pieces = list(pieces) + [out[0]]
        pieces += [swap(out[d], "span", d) for d in (1, 2, 3)]
    query_grad, key_grad, value_grad = unpack(me, pieces, rows, width)
    if not fast:
        head_dim = width // HEADS
        mine = jnp.concatenate(pieces_w, axis=0).reshape(ROW, 1, head_dim, width)
        full = jnp.zeros((ROW, ROW, head_dim, width), BF16)
        full = lax.dynamic_update_slice(full, mine, (0, r, 0, 0)).reshape(width, width)
        weight_grad = lax.psum_scatter(full.astype(F32), "span", scatter_dimension=0, tiled=True)
    return (query_grad, key_grad, value_grad, weight_grad)


def solution(mesh):
    spec = P(("groups", "span"), None)
    return jax.shard_map(
        shards,
        mesh=mesh,
        in_specs=(spec, spec, spec, spec, P(), spec),
        out_specs=(spec, spec, spec, spec),
        check_vma=False,
    )
```

```python
import functools

import jax
import jax.numpy as jnp
from jax import lax
from jax.experimental import pallas as pl
from jax.experimental.pallas import tpu as pltpu
from jax.sharding import PartitionSpec as P

HEADS = 16
BLOCK = 128
WINDOW = 8
ROW = 4
LANES = 128
NEG = -1e30
COUNTS = 24
SPARE, ZERO, SLOTS = 24, 28, 29
VMEM_LIMIT = 16 * 1024 * 1024
SMALL = pl.CostEstimate(flops=1_000_000, bytes_accessed=100_000, transcendentals=0)

F32 = jnp.float32
BF16 = jnp.bfloat16

ANY = pl.BlockSpec(memory_space=pl.ANY)
SMEM = pl.BlockSpec(memory_space=pltpu.SMEM)
VMEM = pl.BlockSpec(memory_space=pltpu.VMEM)


def nn(a, b):
    return lax.dot_general(a, b, (((1,), (0,)), ((), ())), preferred_element_type=F32)


def nt(a, b):
    return lax.dot_general(a, b, (((1,), (1,)), ((), ())), preferred_element_type=F32)


def tn(a, b):
    return lax.dot_general(a, b, (((0,), (0,)), ((), ())), preferred_element_type=F32)


def place():
    index = lax.axis_index("span").astype(jnp.int32)
    return index % ROW, index // ROW


def params():
    return pltpu.CompilerParams(vmem_limit_bytes=VMEM_LIMIT)


def split_pair(a, b):
    lane = lax.broadcasted_iota(jnp.int32, a.shape, 1)
    low = lane < LANES // 2
    even = jnp.where(low, a, pltpu.roll(b, LANES // 2, 1))
    odd = jnp.where(low, pltpu.roll(a, LANES // 2, 1), b)
    return even, odd


def packed(src, chunk, pair):
    r, _ = place()
    odd_me = (r % 2) == 1
    tile = 4 * chunk + (r // 2 + pair) % 2
    a = src[:, pl.ds(pl.multiple_of(tile * LANES, LANES), LANES)].astype(F32)
    b = src[:, pl.ds(pl.multiple_of((tile + 2) * LANES, LANES), LANES)].astype(F32)
    even, odd = split_pair(a, b)
    return jnp.where(odd_me, odd, even), jnp.where(odd_me, even, odd)


def pack_first_kernel(t_v, k_v, v_v, own_ref, o1, o2, o3):
    outs = (o1, o2, o3)
    rows = k_v.shape[0]
    for out in outs:
        out[2 * rows : 2 * rows + 16, :] = jnp.zeros((16, LANES), BF16)
        out[2 * rows : 2 * rows + t_v.shape[0], 0 : t_v.shape[1]] = t_v[...].astype(F32).astype(BF16)
    for which, src in enumerate((k_v, v_v)):
        for side, value in enumerate(packed(src, 1, 0)):
            if side == 0:
                base = (2 + which) * rows
                own_ref[base : base + rows, :] = value.astype(BF16)
        for pair in (0, 1):
            for side, value in enumerate(packed(src, 0, pair)):
                d = 2 * pair + side
                value = value.astype(BF16)
                base = which * rows
                if d == 0:
                    own_ref[base : base + rows, :] = value
                else:
                    outs[d - 1][base : base + rows, :] = value


def pack_second_kernel(q_ref, k_ref, v_ref, *outs):
    rows = k_ref.shape[0]
    for pair in (0, 1):
        for which, src in enumerate((k_ref, v_ref)):
            for side, value in enumerate(packed(src, 1, pair)):
                outs[2 * pair + side][which * rows : (which + 1) * rows, :] = value.astype(BF16)
        for chunk in (0, 1):
            for side, value in enumerate(packed(q_ref, chunk, pair)):
                base = (2 + chunk) * rows
                outs[2 * pair + side][base : base + rows, :] = (value * 0.125).astype(BF16)


def pack_first(track, keys, values):
    rows = keys.shape[0]
    outs = pl.pallas_call(
        pack_first_kernel,
        out_shape=(jax.ShapeDtypeStruct((4 * rows, LANES), BF16),)
        + (jax.ShapeDtypeStruct((2 * rows + 16, LANES), BF16),) * 3,
        in_specs=[VMEM] * 3,
        out_specs=[VMEM] * 4,
        compiler_params=params(),
        cost_estimate=SMALL,
        name="pack_first",
    )(track, keys, values)
    return outs[0], outs[1:]


def pack_second(queries, keys, values):
    rows = queries.shape[0]
    return pl.pallas_call(
        pack_second_kernel,
        out_shape=(jax.ShapeDtypeStruct((4 * rows, LANES), BF16),) * ROW,
        in_specs=[VMEM] * 3,
        out_specs=[VMEM] * ROW,
        compiler_params=params(),
        cost_estimate=SMALL,
        name="pack_second",
    )(queries, keys, values)


def stack_kernel(rows, a, b, c, out):
    for i, src in enumerate((a, b, c)):
        out[i * rows : (i + 1) * rows, :] = src[0:rows, :]


def stack(rows, pieces):
    return pl.pallas_call(
        functools.partial(stack_kernel, rows),
        out_shape=jax.ShapeDtypeStruct((3 * rows, LANES), BF16),
        in_specs=[VMEM] * 3,
        out_specs=VMEM,
        compiler_params=params(),
        cost_estimate=SMALL,
        name="stack",
    )(*pieces)


def grad_kernel(w, g0, g1, g2, g3, out, wide_w, sem):
    r, _ = place()
    half = LANES // 2
    rows = g0.shape[0]
    copies = [
        pltpu.make_async_copy(
            w.at[pl.ds(pl.multiple_of((ROW * j + r) * half, half), half)],
            wide_w.at[pl.ds(j * half, half)],
            sem.at[j],
        )
        for j in range(ROW)
    ]
    for copy in copies:
        copy.start()
    for copy in copies:
        copy.wait()
    for d, g in enumerate((g0, g1, g2, g3)):
        at = pl.multiple_of((r ^ d) * rows, rows)
        out[pl.ds(at, rows), :] = nt(g[...], wide_w[...]).astype(BF16)


def grad_attn(weight, gos):
    rows, width = gos[0].shape
    return pl.pallas_call(
        grad_kernel,
        out_shape=jax.ShapeDtypeStruct((ROW * rows, 2 * LANES), BF16),
        in_specs=[ANY] + [VMEM] * ROW,
        out_specs=VMEM,
        scratch_shapes=[pltpu.VMEM((2 * LANES, width), BF16), pltpu.SemaphoreType.DMA((ROW,))],
        compiler_params=params(),
        cost_estimate=SMALL,
        name="grad_attn",
    )(weight, *gos)


def plan_kernel(track_ref, list_ref):
    r, z = place()

    def one_query(qi, carry):
        rho = qi // 2
        span = ROW * z + rho
        source = 2 * (r ^ rho) + qi % 2

        near, total = jnp.int32(0), jnp.int32(0)
        for i in range(2 * WINDOW):
            u = span - (i // 2 + 1)
            use = jnp.logical_and(track_ref[source, i] == 1, u >= 0).astype(jnp.int32)
            safe = jnp.maximum(u, 0)
            back = z - safe // ROW
            list_ref[qi, total] = (back * ROW + safe % ROW) * 2 + i % 2
            near = near + jnp.where(back < 2, use, 0)
            total = total + use
        list_ref[qi, COUNTS] = near
        list_ref[qi, COUNTS + 1] = total
        return carry

    lax.fori_loop(0, 2 * ROW, one_query, 0)


def plan(track_row):
    return pl.pallas_call(
        plan_kernel,
        out_shape=jax.ShapeDtypeStruct((2 * ROW, COUNTS + 2), jnp.int32),
        in_specs=[SMEM],
        out_specs=SMEM,
        cost_estimate=SMALL,
        name="plan",
    )(track_row)


def low_lanes(shape):
    return lax.broadcasted_iota(jnp.int32, shape, 1) < LANES // 2


def two_heads(x):
    low, zero = low_lanes(x.shape), jnp.zeros_like(x)
    return jnp.concatenate([jnp.where(low, x, zero), jnp.where(low, zero, x)], axis=0)


def pick(x):
    return jnp.where(low_lanes((BLOCK, LANES)), x[:BLOCK], x[BLOCK:])


def causal(shape):
    query = lax.broadcasted_iota(jnp.int32, shape, 0) % BLOCK
    return lax.broadcasted_iota(jnp.int32, shape, 1) <= query


def row_copies(r, chunk, back, own, rest, kk, vv, sem, slot):
    out = []
    for d in range(ROW):
        src, base = (own, 512 * chunk) if d == 0 else (rest, 512 * (d - 1))
        place = pl.ds(8 * back + 2 * (r ^ d), 2)
        keys = src.at[pl.ds(base, 256)].reshape(2, BLOCK, LANES)
        values = src.at[pl.ds(base + 256, 256)].reshape(2, BLOCK, LANES)
        at = slot + 2 * d
        out.append(pltpu.make_async_copy(keys, kk.at[place], sem.at[at]))
        out.append(
            pltpu.make_async_copy(values, vv.at[place, :, pl.ds(0, LANES)], sem.at[at + 1])
        )
    return out


def query_copies(r, chunk, seconds, qq, sem, slot):
    out = []
    for d, second in enumerate(seconds):
        blocks = second.at[pl.ds(512 + chunk * 256, 256)].reshape(2, BLOCK, LANES)
        out.append(pltpu.make_async_copy(blocks, qq.at[pl.ds(2 * (r ^ d), 2)], sem.at[slot + d]))
    return out


def slots_of(list_ref, qi, start, count, how_many):
    ks, vs = [], []
    for i in range(how_many):
        position = start + i
        inside = position < count
        f = list_ref[qi, jnp.minimum(position, COUNTS - 1)]
        ks.append(jnp.where(inside, f, SPARE + qi // 2))
        vs.append(jnp.where(inside, f, ZERO))
    return ks, vs


def own_slots(rho, b):
    return [2 * rho if b else SPARE + rho, 2 * rho + b], [2 * rho if b else ZERO, 2 * rho + b]


def fwd_group(kk, vv, q2, ks, vs, diag=None):
    scores = nt(q2, jnp.concatenate([kk[f] for f in ks], axis=0))
    parts = [scores[:, i * BLOCK : (i + 1) * BLOCK] for i in range(len(ks))]
    if diag is not None:
        parts[diag] = jnp.where(causal(parts[diag].shape), parts[diag], NEG)
    top = jnp.max(functools.reduce(jnp.maximum, parts), axis=1, keepdims=True)
    expo = jnp.concatenate([jnp.exp(part - top).astype(BF16) for part in parts], axis=1)
    out = nn(expo, jnp.concatenate([vv[f] for f in vs], axis=0))
    return pick(jnp.broadcast_to(top, (2 * BLOCK, LANES))), pick(out[:, LANES:]), pick(out[:, :LANES])


def merge(before, state, qi, group):
    m, l, num = before[0, qi], before[1, qi], before[2, qi]
    top = jnp.maximum(m, group[0])
    old, new = jnp.exp(m - top), jnp.exp(group[0] - top)
    state[0, qi] = top
    state[1, qi] = l * old + group[1] * new
    state[2, qi] = num * old + group[2] * new


NEAR_FIRST = (6, 6, 8, 8)
FAR_FIRST = (6, 4, 4, 2)
BACK_FIRST = 10


def near_kernel(
    chunk, list_ref, own0, rest0, own1, rest1, s0, s1, s2, s3, after, state, kk, vv, qq, sem
):
    r, _ = place()
    copies = row_copies(r, chunk, 0, own0, rest0, kk, vv, sem, 0)
    copies += row_copies(r, chunk, 1, own1, rest1, kk, vv, sem, 8)
    copies += query_copies(r, chunk, (s0, s1, s2, s3), qq, sem, 16)
    for copy in copies:
        copy.start()
    kk[ZERO] = jnp.zeros((BLOCK, LANES), BF16)
    for f in range(SLOTS):
        if f < SPARE:
            vv[f, :, LANES : 2 * LANES] = jnp.ones((BLOCK, LANES), BF16)
        else:
            vv[f] = jnp.zeros((BLOCK, 2 * LANES), BF16)
    for copy in copies:
        copy.wait()
    for rho in range(ROW):
        kk[SPARE + rho] = jnp.broadcast_to(kk[2 * rho, 0:1, :], (BLOCK, LANES))
    for qi in range(2 * ROW):
        rho, b = qi // 2, qi % 2
        ks, vs = slots_of(list_ref, qi, 0, list_ref[qi, COUNTS], NEAR_FIRST[rho])
        own_ks, own_vs = own_slots(rho, b)
        group = fwd_group(kk, vv, two_heads(qq[qi]), own_ks + ks, own_vs + vs, diag=1)
        for i, value in enumerate(group):
            state[i, qi] = value
    for rho in range(ROW):
        counts = [list_ref[2 * rho + b, COUNTS] for b in (0, 1)]
        first = NEAR_FIRST[rho]

        def body(g, carry):
            for b in (0, 1):
                qi = 2 * rho + b
                ks, vs = slots_of(list_ref, qi, first + 4 * g, counts[b], 4)
                merge(state, state, qi, fwd_group(kk, vv, two_heads(qq[qi]), ks, vs))
            return carry

        lax.fori_loop(0, (jnp.maximum(counts[0], counts[1]) - first + 3) // 4, body, 0)


def near(chunk, lists, own0, rest0, own1, rest1, seconds, after):
    return pl.pallas_call(
        functools.partial(near_kernel, chunk),
        out_shape=(
            jax.ShapeDtypeStruct((3, 8, BLOCK, LANES), F32),
            jax.ShapeDtypeStruct((SLOTS, BLOCK, LANES), BF16),
            jax.ShapeDtypeStruct((SLOTS, BLOCK, 2 * LANES), BF16),
            jax.ShapeDtypeStruct((8, BLOCK, LANES), BF16),
        ),
        in_specs=[SMEM] + [ANY] * 9,
        out_specs=[VMEM] * 4,
        scratch_shapes=[pltpu.SemaphoreType.DMA((20,))],
        compiler_params=params(),
        cost_estimate=SMALL,
        name=f"near{chunk}",
    )(lists, own0, rest0, own1, rest1, *seconds, after)


def far_kernel(
    chunk, last, list_ref, own2, rest2, g0, g1, g2, g3, after, earlier, state_in, kk_in, vv_in, qq,
    kk, vv, attn_ref, lse_ref, *refs
):
    *terms, state, wide, sem = refs
    r, z = place()
    copies = row_copies(r, chunk, 2, own2, rest2, kk, vv, sem, 0)
    for copy in copies:
        copy.start()
    late = pltpu.make_async_copy(earlier, wide.at[pl.ds(0, LANES)], sem.at[8]) if last else None
    if last:
        late.start()
    for copy in copies:
        copy.wait()
    for qi in range(2 * ROW):
        ks, vs = slots_of(
            list_ref, qi, list_ref[qi, COUNTS], list_ref[qi, COUNTS + 1], FAR_FIRST[qi // 2]
        )
        group = fwd_group(kk, vv, two_heads(qq[qi]), ks, vs)
        merge(state_in, state, qi, group)
    for rho in range(ROW):
        starts = [list_ref[2 * rho + b, COUNTS] + FAR_FIRST[rho] for b in (0, 1)]
        counts = [list_ref[2 * rho + b, COUNTS + 1] for b in (0, 1)]

        def body(g, carry):
            for b in (0, 1):
                qi = 2 * rho + b
                ks, vs = slots_of(list_ref, qi, starts[b] + 4 * g, counts[b], 4)
                merge(state, state, qi, fwd_group(kk, vv, two_heads(qq[qi]), ks, vs))
            return carry

        longest = jnp.maximum(counts[0] - starts[0], counts[1] - starts[1])
        lax.fori_loop(0, (longest + 3) // 4, body, 0)
    for qi in range(2 * ROW):
        lse_ref[qi] = state[0, qi] + jnp.log(state[1, qi])
        attn_ref[qi * BLOCK : (qi + 1) * BLOCK, :] = (state[2, qi] / state[1, qi]).astype(BF16)
    term = None
    for d, g in enumerate((g0, g1, g2, g3)):
        rows = g.shape[0]
        at = pl.multiple_of((r ^ d) * rows, rows)
        part = tn(attn_ref[pl.ds(at, rows), :], g[...])
        term = part if term is None else term + part
    if not last:
        terms[0][...] = term.astype(BF16)
        return
    late.wait()
    wide[LANES : 2 * LANES, :] = term.astype(BF16)
    half = LANES // 2
    for delta, out in enumerate(terms):
        at = pl.multiple_of((z + delta) % ROW * half, half)
        out[...] = wide[pl.ds(at, half), :]


def far(chunk, last, lists, own2, rest2, gos, after, earlier, state, kk, vv, qq):
    width = gos[0].shape[1]
    weights = (
        (jax.ShapeDtypeStruct((LANES // 2, width), BF16),) * 4
        if last
        else (jax.ShapeDtypeStruct((LANES, width), BF16),)
    )
    return pl.pallas_call(
        functools.partial(far_kernel, chunk, last),
        out_shape=(
            jax.ShapeDtypeStruct(kk.shape, BF16),
            jax.ShapeDtypeStruct(vv.shape, BF16),
            jax.ShapeDtypeStruct((8 * BLOCK, LANES), BF16),
            jax.ShapeDtypeStruct((8, BLOCK, LANES), F32),
        )
        + weights,
        in_specs=[SMEM] + [ANY] * 2 + [VMEM] * ROW + [ANY] * 2 + [VMEM] * 4,
        out_specs=[VMEM] * (4 + len(weights)),
        input_output_aliases={10: 0, 11: 1},
        scratch_shapes=[
            pltpu.VMEM((3, 8, BLOCK, LANES), F32),
            pltpu.VMEM((2 * LANES, width), BF16),
            pltpu.SemaphoreType.DMA((9,)),
        ],
        compiler_params=params(),
        cost_estimate=SMALL,
        name=f"far{chunk}",
    )(lists, own2, rest2, *gos, after, earlier, state, kk, vv, qq)


def bwd_group(kk, vv, q2, g2, lse, delta, ks, vs, diag=None):
    scores = nt(q2, jnp.concatenate([kk[f] for f in ks], axis=0))
    dprob = nt(g2, jnp.concatenate([vv[f, :, 0:LANES] for f in ks], axis=0))
    probs, dscores = [], []
    for i in range(len(ks)):
        part = scores[:, i * BLOCK : (i + 1) * BLOCK]
        if diag == i:
            part = jnp.where(causal(part.shape), part, NEG)
        prob = jnp.exp(part - lse)
        dscores.append((prob * (dprob[:, i * BLOCK : (i + 1) * BLOCK] - delta)).astype(BF16))
        probs.append(prob)
    out = nn(jnp.concatenate(dscores, axis=1), jnp.concatenate([kk[f] for f in vs], axis=0))
    return probs, dscores, out


def back_kernel(chunk, which_d, list_ref, kk, vv, qq, g_ref, attn_ref, lse_ref, after, *refs):
    *outs, dq = refs
    r, _ = place()

    def query_side(qi):
        at = pl.ds(pl.multiple_of(qi * BLOCK, BLOCK), BLOCK)
        g = g_ref[at, chunk * LANES : (chunk + 1) * LANES]
        product = g.astype(F32) * attn_ref[at, :].astype(F32)
        low = low_lanes(product.shape)
        delta = jnp.concatenate(
            [
                jnp.sum(jnp.where(low, product, 0.0), axis=1, keepdims=True),
                jnp.sum(jnp.where(low, 0.0, product), axis=1, keepdims=True),
            ],
            axis=0,
        )
        half = LANES // 2
        lse = jnp.concatenate([lse_ref[qi, :, 0:1], lse_ref[qi, :, half : half + 1]], axis=0)
        return two_heads(qq[qi]), two_heads(g), lse, delta

    for n, d in enumerate(which_d):
        rho = r ^ d
        sides = [query_side(2 * rho + b) for b in (0, 1)]
        local = []
        for b in (0, 1):
            qi = 2 * rho + b
            ks, vs = slots_of(list_ref, qi, 0, list_ref[qi, COUNTS + 1], BACK_FIRST)
            own_ks, own_vs = own_slots(rho, b)
            probs, dscores, add = bwd_group(kk, vv, *sides[b], own_ks + ks, own_vs + vs, diag=1)
            dq[2 * n + b] = add
            local.append(([p.astype(BF16) for p in probs[:2]], dscores[:2]))
        out = outs[n]
        for which, side in ((1, 0), (0, 1)):
            both = jnp.concatenate([sides[0][side], sides[1][side]], axis=0)
            first = jnp.concatenate([local[0][which][1], local[1][which][0]], axis=0)
            base = 512 if side else 256
            out[base : base + BLOCK, :] = tn(first, both).astype(BF16)
            out[base + BLOCK : base + 256, :] = tn(local[1][which][1], sides[1][side]).astype(BF16)
    for n, d in enumerate(which_d):
        rho = r ^ d
        counts = [list_ref[2 * rho + b, COUNTS + 1] for b in (0, 1)]

        def body(g, carry):
            for b in (0, 1):
                qi = 2 * rho + b
                ks, vs = slots_of(list_ref, qi, BACK_FIRST + 4 * g, counts[b], 4)
                _, _, add = bwd_group(kk, vv, *query_side(qi), ks, vs)
                dq[2 * n + b] += add
            return carry

        lax.fori_loop(0, (jnp.maximum(counts[0], counts[1]) - BACK_FIRST + 3) // 4, body, 0)
    for n in range(len(which_d)):
        for b in (0, 1):
            outs[n][b * BLOCK : (b + 1) * BLOCK, :] = (pick(dq[2 * n + b]) * 0.125).astype(BF16)


def back(chunk, which_d, lists, kk, vv, qq, grads, attn, lse, after):
    return pl.pallas_call(
        functools.partial(back_kernel, chunk, which_d),
        out_shape=(jax.ShapeDtypeStruct((768, LANES), BF16),) * len(which_d),
        in_specs=[SMEM] + [VMEM] * 6 + [ANY],
        out_specs=[VMEM] * len(which_d),
        scratch_shapes=[pltpu.VMEM((2 * len(which_d), 2 * BLOCK, LANES), F32)],
        compiler_params=params(),
        cost_estimate=SMALL,
        name=f"back{chunk}_{which_d[0]}",
    )(lists, kk, vv, qq, grads, attn, lse, after)


def unpack_kernel(chunk, *refs):
    ins, outs = refs[:ROW], refs[-3:]
    r, _ = place()
    odd_me = (r % 2) == 1
    rows, width = outs[0].shape
    for pair in (0, 1):
        tile = (r // 2 + pair) % 2
        first, second = ins[2 * pair], ins[2 * pair + 1]
        for which, out in enumerate(outs):
            a = first[which * rows : (which + 1) * rows, :].astype(F32)
            b = second[which * rows : (which + 1) * rows, :].astype(F32)
            low, high = jnp.where(odd_me, b, a), jnp.where(odd_me, a, b)
            one, two = split_pair(low, high)
            out[:, pl.ds(pl.multiple_of(tile * LANES, LANES), LANES)] = one.astype(BF16)
            out[:, pl.ds(pl.multiple_of((tile + 2) * LANES, LANES), LANES)] = two.astype(BF16)


def unpack(chunk, pieces, rows, width, before):
    half = pl.BlockSpec((rows, width // 2), lambda i: (0, chunk))
    return pl.pallas_call(
        functools.partial(unpack_kernel, chunk),
        grid=(1,),
        out_shape=(jax.ShapeDtypeStruct((rows, width), BF16),) * 3,
        in_specs=[VMEM] * ROW + [ANY] * len(before),
        out_specs=[half] * 3,
        input_output_aliases={ROW + i: i for i in range(len(before))},
        compiler_params=params(),
        cost_estimate=SMALL,
        name=f"unpack{chunk}",
    )(*pieces, *before)


def swap(value, axis, bit):
    count = lax.axis_size(axis)
    return lax.ppermute(value, axis, [(s, s ^ bit) for s in range(count)])


def later(value, axis):
    count = lax.axis_size(axis)
    return lax.ppermute(value, axis, [(s, (s + ROW) % count) for s in range(count)])


hold = lax.optimization_barrier


def shards(queries, keys, values, track, out_weight, grad_out):
    rows, width = queries.shape
    count = lax.axis_size("span")
    fast = count == HEADS

    own0, firsts = pack_first(track, keys, values)
    own1 = later(own0, "span")
    got_first = [swap(x, "span", d + 1) for d, x in enumerate(firsts)]
    queries, _ = hold((queries, got_first[0]))
    seconds = list(pack_second(queries, keys, values))
    got_first, _ = hold((got_first, seconds[0]))
    rest0 = [stack(2 * rows, got_first)]
    rest1 = [later(rest0[0], "span")]
    track_row = jnp.concatenate(
        [track.astype(BF16)] + [x[2 * rows : 2 * rows + 2, : 2 * WINDOW] for x in got_first], axis=0
    )
    lists = plan(track_row.astype(jnp.int32))

    seconds, _ = hold((seconds, (rest0[0], own1)))
    seconds[1:] = [swap(seconds[d], "span", d) for d in (1, 2, 3)]
    own2 = later(own1, "span")
    arrived, _ = hold((seconds[1:], (rest1[0], own2, lists)))
    rest0.append(stack(2 * rows, arrived))
    rest1.append(later(rest0[1], "span"))
    grad_late, _ = hold((grad_out, rest0[1]))
    go2 = swap(grad_late, "span", 2)

    stores = [near(0, lists, own0, rest0[0], own1, rest1[0], seconds, lists)]
    first_row, _ = hold((rest1[0], stores[0][0]))
    rest2 = [later(first_row, "span"), later(rest1[1], "span")]
    (grad_late, go2), _ = hold(((grad_out, go2), (stores[0][0], rest1[1])))
    gos = (grad_out, swap(grad_late, "span", 1), go2, swap(go2, "span", 1))
    grads = grad_attn(out_weight, gos)
    stores.append(near(1, lists, own0, rest0[1], own1, rest1[1], seconds, stores[0][0]))

    after = stores[1][0]
    kk, vv, attn, lse, term = far(0, False, lists, own2, rest2[0], gos, after, after, *stores[0])
    out = back(0, (0, 1, 2, 3), lists, kk, vv, stores[0][3], grads, attn, lse, attn)
    pieces = [out[0]] + [swap(out[d], "span", d) for d in (1, 2, 3)]
    grads_out = unpack(0, pieces, rows, width, ())

    kk, vv, attn, lse, *terms = far(1, fast, lists, own2, rest2[1], gos, out[0], term, *stores[1])
    second = (lists, kk, vv, stores[1][3], grads, attn, lse)
    if fast:
        weight_grad = terms[0].astype(F32)
        for delta in (1, 2, 3):
            pairs = [
                (ROW * s + q, ROW * ((s + delta) % ROW) + q) for s in range(ROW) for q in range(ROW)
            ]
            weight_grad += lax.ppermute(terms[delta], "span", pairs).astype(F32)
    else:
        head_dim = width // HEADS
        place_in_row = lax.axis_index("span").astype(jnp.int32) % ROW
        mine = jnp.concatenate([term, terms[0]], axis=0).reshape(ROW, 1, head_dim, width)
        full = jnp.zeros((ROW, ROW, head_dim, width), BF16)
        full = lax.dynamic_update_slice(full, mine, (0, place_in_row, 0, 0)).reshape(width, width)
        weight_grad = lax.psum_scatter(full.astype(F32), "span", scatter_dimension=0, tiled=True)
    out = back(1, (2, 3, 1), *second, attn)
    out, grads_out = hold((out, grads_out))
    crossed = [swap(x, "span", d) for x, d in zip(out, (2, 3, 1))]
    (own,) = back(1, (0,), *second, out[0])
    pieces = [own, crossed[2], crossed[0], crossed[1]]
    query_grad, key_grad, value_grad = unpack(1, pieces, rows, width, grads_out)
    return (query_grad, key_grad, value_grad, weight_grad)


def solution(mesh):
    spec = P(("groups", "span"), None)
    return jax.shard_map(
        shards,
        mesh=mesh,
        in_specs=(spec, spec, spec, spec, P(), spec),
        out_specs=(spec, spec, spec, spec),
        check_vma=False,
    )
```

```python
import functools

import jax
import jax.numpy as jnp
from jax import lax
from jax.experimental import pallas as pl
from jax.experimental.pallas import tpu as pltpu
from jax.sharding import PartitionSpec as P

HEADS = 16
BLOCK = 128
WINDOW = 8
ROW = 4
LANES = 128
NEG = -1e30
COUNTS = 24
SPARE, ZERO, SLOTS = 24, 28, 29
VMEM_LIMIT = 16 * 1024 * 1024
SMALL = pl.CostEstimate(flops=1_000_000, bytes_accessed=100_000, transcendentals=0)

F32 = jnp.float32
BF16 = jnp.bfloat16

ANY = pl.BlockSpec(memory_space=pl.ANY)
SMEM = pl.BlockSpec(memory_space=pltpu.SMEM)
VMEM = pl.BlockSpec(memory_space=pltpu.VMEM)


def nn(a, b):
    return lax.dot_general(a, b, (((1,), (0,)), ((), ())), preferred_element_type=F32)


def nt(a, b):
    return lax.dot_general(a, b, (((1,), (1,)), ((), ())), preferred_element_type=F32)


def tn(a, b):
    return lax.dot_general(a, b, (((0,), (0,)), ((), ())), preferred_element_type=F32)


def place():
    index = lax.axis_index("span").astype(jnp.int32)
    return index % ROW, index // ROW


def params():
    return pltpu.CompilerParams(vmem_limit_bytes=VMEM_LIMIT)


def split_pair(a, b):
    lane = lax.broadcasted_iota(jnp.int32, a.shape, 1)
    low = lane < LANES // 2
    even = jnp.where(low, a, pltpu.roll(b, LANES // 2, 1))
    odd = jnp.where(low, pltpu.roll(a, LANES // 2, 1), b)
    return even, odd


def packed(src, chunk, pair):
    r, _ = place()
    odd_me = (r % 2) == 1
    tile = 4 * chunk + (r // 2 + pair) % 2
    a = src[:, pl.ds(pl.multiple_of(tile * LANES, LANES), LANES)].astype(F32)
    b = src[:, pl.ds(pl.multiple_of((tile + 2) * LANES, LANES), LANES)].astype(F32)
    even, odd = split_pair(a, b)
    return jnp.where(odd_me, odd, even), jnp.where(odd_me, even, odd)


def pack_first_kernel(t_v, k_v, v_v, own_ref, o1, o2, o3):
    outs = (o1, o2, o3)
    rows = k_v.shape[0]
    for out in outs:
        out[2 * rows : 2 * rows + 16, :] = jnp.zeros((16, LANES), BF16)
        out[2 * rows : 2 * rows + t_v.shape[0], 0 : t_v.shape[1]] = t_v[...].astype(F32).astype(BF16)
    for which, src in enumerate((k_v, v_v)):
        for side, value in enumerate(packed(src, 1, 0)):
            if side == 0:
                base = (2 + which) * rows
                own_ref[base : base + rows, :] = value.astype(BF16)
        for pair in (0, 1):
            for side, value in enumerate(packed(src, 0, pair)):
                d = 2 * pair + side
                value = value.astype(BF16)
                base = which * rows
                if d == 0:
                    own_ref[base : base + rows, :] = value
                else:
                    outs[d - 1][base : base + rows, :] = value


def pack_second_kernel(q_ref, k_ref, v_ref, *outs):
    rows = k_ref.shape[0]
    for pair in (0, 1):
        for which, src in enumerate((k_ref, v_ref)):
            for side, value in enumerate(packed(src, 1, pair)):
                outs[2 * pair + side][which * rows : (which + 1) * rows, :] = value.astype(BF16)
        for chunk in (0, 1):
            for side, value in enumerate(packed(q_ref, chunk, pair)):
                base = (2 + chunk) * rows
                outs[2 * pair + side][base : base + rows, :] = (value * 0.125).astype(BF16)


def pack_first(track, keys, values):
    rows = keys.shape[0]
    outs = pl.pallas_call(
        pack_first_kernel,
        out_shape=(jax.ShapeDtypeStruct((4 * rows, LANES), BF16),)
        + (jax.ShapeDtypeStruct((2 * rows + 16, LANES), BF16),) * 3,
        in_specs=[VMEM] * 3,
        out_specs=[VMEM] * 4,
        compiler_params=params(),
        cost_estimate=SMALL,
        name="pack_first",
    )(track, keys, values)
    return outs[0], outs[1:]


def pack_second(queries, keys, values):
    rows = queries.shape[0]
    return pl.pallas_call(
        pack_second_kernel,
        out_shape=(jax.ShapeDtypeStruct((4 * rows, LANES), BF16),) * ROW,
        in_specs=[VMEM] * 3,
        out_specs=[VMEM] * ROW,
        compiler_params=params(),
        cost_estimate=SMALL,
        name="pack_second",
    )(queries, keys, values)


def stack_kernel(rows, a, b, c, out):
    for i, src in enumerate((a, b, c)):
        out[i * rows : (i + 1) * rows, :] = src[0:rows, :]


def stack(rows, pieces):
    return pl.pallas_call(
        functools.partial(stack_kernel, rows),
        out_shape=jax.ShapeDtypeStruct((3 * rows, LANES), BF16),
        in_specs=[VMEM] * 3,
        out_specs=VMEM,
        compiler_params=params(),
        cost_estimate=SMALL,
        name="stack",
    )(*pieces)


def grad_kernel(w, g0, g1, g2, g3, out, wide_w):
    r, _ = place()
    half = LANES // 2
    rows = g0.shape[0]
    for j in range(ROW):
        at = pl.multiple_of((ROW * j + r) * half, half)
        wide_w[j * half : (j + 1) * half, :] = w[pl.ds(at, half), :]
    for d, g in enumerate((g0, g1, g2, g3)):
        at = pl.multiple_of((r ^ d) * rows, rows)
        out[pl.ds(at, rows), :] = nt(g[...], wide_w[...]).astype(BF16)


def grad_attn(weight, gos):
    rows, width = gos[0].shape
    return pl.pallas_call(
        grad_kernel,
        out_shape=jax.ShapeDtypeStruct((ROW * rows, 2 * LANES), BF16),
        in_specs=[VMEM] * (1 + ROW),
        out_specs=VMEM,
        scratch_shapes=[pltpu.VMEM((2 * LANES, width), BF16)],
        compiler_params=params(),
        cost_estimate=SMALL,
        name="grad_attn",
    )(weight, *gos)


def plan_kernel(track_ref, list_ref):
    r, z = place()

    def one_query(qi, carry):
        rho = qi // 2
        span = ROW * z + rho
        source = 2 * (r ^ rho) + qi % 2

        near, total = jnp.int32(0), jnp.int32(0)
        for i in range(2 * WINDOW):
            u = span - (i // 2 + 1)
            use = jnp.logical_and(track_ref[source, i] == 1, u >= 0).astype(jnp.int32)
            safe = jnp.maximum(u, 0)
            back = z - safe // ROW
            list_ref[qi, total] = (back * ROW + safe % ROW) * 2 + i % 2
            near = near + jnp.where(back < 2, use, 0)
            total = total + use
        list_ref[qi, COUNTS] = near
        list_ref[qi, COUNTS + 1] = total
        return carry

    lax.fori_loop(0, 2 * ROW, one_query, 0)


def plan(track_row):
    return pl.pallas_call(
        plan_kernel,
        out_shape=jax.ShapeDtypeStruct((2 * ROW, COUNTS + 2), jnp.int32),
        in_specs=[SMEM],
        out_specs=SMEM,
        cost_estimate=SMALL,
        name="plan",
    )(track_row)


def low_lanes(shape):
    return lax.broadcasted_iota(jnp.int32, shape, 1) < LANES // 2


def two_heads(x):
    low, zero = low_lanes(x.shape), jnp.zeros_like(x)
    return jnp.concatenate([jnp.where(low, x, zero), jnp.where(low, zero, x)], axis=0)


def pick(x):
    return jnp.where(low_lanes((BLOCK, LANES)), x[:BLOCK], x[BLOCK:])


def causal(shape):
    query = lax.broadcasted_iota(jnp.int32, shape, 0) % BLOCK
    return lax.broadcasted_iota(jnp.int32, shape, 1) <= query


def gather_row(r, chunk, back, own, rest, kk, vv):
    for d in range(ROW):
        src, base = (own, 512 * chunk) if d == 0 else (rest, 512 * (d - 1))
        for b in (0, 1):
            f = 8 * back + 2 * (r ^ d) + b
            at = base + b * BLOCK
            kk[f] = src[at : at + BLOCK, :]
            vv[f, :, 0:LANES] = src[at + 256 : at + 256 + BLOCK, :]


def gather_queries(r, chunk, seconds, qq):
    for d, second in enumerate(seconds):
        for b in (0, 1):
            at = 512 + chunk * 256 + b * BLOCK
            qq[2 * (r ^ d) + b] = second[at : at + BLOCK, :]


def slots_of(list_ref, qi, start, count, how_many):
    ks, vs = [], []
    for i in range(how_many):
        position = start + i
        inside = position < count
        f = list_ref[qi, jnp.minimum(position, COUNTS - 1)]
        ks.append(jnp.where(inside, f, SPARE + qi // 2))
        vs.append(jnp.where(inside, f, ZERO))
    return ks, vs


def own_slots(rho, b):
    return [2 * rho if b else SPARE + rho, 2 * rho + b], [2 * rho if b else ZERO, 2 * rho + b]


def fwd_group(kk, vv, q2, ks, vs, diag=None):
    scores = nt(q2, jnp.concatenate([kk[f] for f in ks], axis=0))
    parts = [scores[:, i * BLOCK : (i + 1) * BLOCK] for i in range(len(ks))]
    if diag is not None:
        parts[diag] = jnp.where(causal(parts[diag].shape), parts[diag], NEG)
    top = jnp.max(functools.reduce(jnp.maximum, parts), axis=1, keepdims=True)
    expo = jnp.concatenate([jnp.exp(part - top).astype(BF16) for part in parts], axis=1)
    out = nn(expo, jnp.concatenate([vv[f] for f in vs], axis=0))
    return pick(jnp.broadcast_to(top, (2 * BLOCK, LANES))), pick(out[:, LANES:]), pick(out[:, :LANES])


def merge(before, state, qi, group):
    m, l, num = before[0, qi], before[1, qi], before[2, qi]
    top = jnp.maximum(m, group[0])
    old, new = jnp.exp(m - top), jnp.exp(group[0] - top)
    state[0, qi] = top
    state[1, qi] = l * old + group[1] * new
    state[2, qi] = num * old + group[2] * new


NEAR_FIRST = tuple(6 + 2 * (rho // 2) for rho in range(ROW))
FAR_FIRST = tuple(6 - 2 * ((rho + 1) // 2) for rho in range(ROW))
BACK_FIRST = 10


def near_kernel(
    chunk, list_ref, own0, rest0, own1, rest1, s0, s1, s2, s3, after, state, kk, vv, qq
):
    r, _ = place()
    gather_row(r, chunk, 0, own0, rest0, kk, vv)
    gather_row(r, chunk, 1, own1, rest1, kk, vv)
    gather_queries(r, chunk, (s0, s1, s2, s3), qq)
    kk[ZERO] = jnp.zeros((BLOCK, LANES), BF16)
    for f in range(SLOTS):
        if f < SPARE:
            vv[f, :, LANES : 2 * LANES] = jnp.ones((BLOCK, LANES), BF16)
        else:
            vv[f] = jnp.zeros((BLOCK, 2 * LANES), BF16)
    for rho in range(ROW):
        kk[SPARE + rho] = jnp.broadcast_to(kk[2 * rho, 0:1, :], (BLOCK, LANES))
    for qi in range(2 * ROW):
        rho, b = qi // 2, qi % 2
        ks, vs = slots_of(list_ref, qi, 0, list_ref[qi, COUNTS], NEAR_FIRST[rho])
        own_ks, own_vs = own_slots(rho, b)
        group = fwd_group(kk, vv, two_heads(qq[qi]), own_ks + ks, own_vs + vs, diag=1)
        for i, value in enumerate(group):
            state[i, qi] = value

    def overflow(rho, carry):
        first = NEAR_FIRST[0] + 2 * (rho // 2)
        counts = [list_ref[2 * rho + b, COUNTS] for b in (0, 1)]

        def body(g, inner):
            for b in (0, 1):
                qi = 2 * rho + b
                ks, vs = slots_of(list_ref, qi, first + 4 * g, counts[b], 4)
                merge(state, state, qi, fwd_group(kk, vv, two_heads(qq[qi]), ks, vs))
            return inner

        return lax.fori_loop(0, (jnp.maximum(counts[0], counts[1]) - first + 3) // 4, body, carry)

    lax.fori_loop(0, ROW, overflow, 0)


def near(chunk, lists, own0, rest0, own1, rest1, seconds, after):
    return pl.pallas_call(
        functools.partial(near_kernel, chunk),
        out_shape=(
            jax.ShapeDtypeStruct((3, 8, BLOCK, LANES), F32),
            jax.ShapeDtypeStruct((SLOTS, BLOCK, LANES), BF16),
            jax.ShapeDtypeStruct((SLOTS, BLOCK, 2 * LANES), BF16),
            jax.ShapeDtypeStruct((8, BLOCK, LANES), BF16),
        ),
        in_specs=[SMEM] + [VMEM] * 8 + [ANY],
        out_specs=[VMEM] * 4,
        compiler_params=params(),
        cost_estimate=SMALL,
        name=f"near{chunk}",
    )(lists, own0, rest0, own1, rest1, *seconds, after)


def far_kernel(
    chunk, last, list_ref, own2, rest2, g0, g1, g2, g3, after, earlier, state_in, kk_in, vv_in, qq,
    kk, vv, attn_ref, lse_ref, *refs
):
    *terms, state, wide = refs
    r, z = place()
    gather_row(r, chunk, 2, own2, rest2, kk, vv)
    for qi in range(2 * ROW):
        ks, vs = slots_of(
            list_ref, qi, list_ref[qi, COUNTS], list_ref[qi, COUNTS + 1], FAR_FIRST[qi // 2]
        )
        group = fwd_group(kk, vv, two_heads(qq[qi]), ks, vs)
        merge(state_in, state, qi, group)

    def overflow(rho, carry):
        first = FAR_FIRST[0] - 2 * ((rho + 1) // 2)
        starts = [list_ref[2 * rho + b, COUNTS] + first for b in (0, 1)]
        counts = [list_ref[2 * rho + b, COUNTS + 1] for b in (0, 1)]

        def body(g, inner):
            for b in (0, 1):
                qi = 2 * rho + b
                ks, vs = slots_of(list_ref, qi, starts[b] + 4 * g, counts[b], 4)
                merge(state, state, qi, fwd_group(kk, vv, two_heads(qq[qi]), ks, vs))
            return inner

        longest = jnp.maximum(counts[0] - starts[0], counts[1] - starts[1])
        return lax.fori_loop(0, (longest + 3) // 4, body, carry)

    lax.fori_loop(0, ROW, overflow, 0)
    for qi in range(2 * ROW):
        lse_ref[qi] = state[0, qi] + jnp.log(state[1, qi])
        attn_ref[qi * BLOCK : (qi + 1) * BLOCK, :] = (state[2, qi] / state[1, qi]).astype(BF16)
    term = None
    for d, g in enumerate((g0, g1, g2, g3)):
        rows = g.shape[0]
        at = pl.multiple_of((r ^ d) * rows, rows)
        part = tn(attn_ref[pl.ds(at, rows), :], g[...])
        term = part if term is None else term + part
    if not last:
        terms[0][...] = term.astype(BF16)
        return
    wide[0:LANES, :] = earlier[...]
    wide[LANES : 2 * LANES, :] = term.astype(BF16)
    half = LANES // 2
    for delta, out in enumerate(terms):
        at = pl.multiple_of((z + delta) % ROW * half, half)
        out[...] = wide[pl.ds(at, half), :]


def far(chunk, last, lists, own2, rest2, gos, after, earlier, state, kk, vv, qq):
    width = gos[0].shape[1]
    weights = (
        (jax.ShapeDtypeStruct((LANES // 2, width), BF16),) * 4
        if last
        else (jax.ShapeDtypeStruct((LANES, width), BF16),)
    )
    return pl.pallas_call(
        functools.partial(far_kernel, chunk, last),
        out_shape=(
            jax.ShapeDtypeStruct(kk.shape, BF16),
            jax.ShapeDtypeStruct(vv.shape, BF16),
            jax.ShapeDtypeStruct((8 * BLOCK, LANES), BF16),
            jax.ShapeDtypeStruct((8, BLOCK, LANES), F32),
        )
        + weights,
        in_specs=[SMEM] + [VMEM] * 2 + [VMEM] * ROW + [ANY, VMEM if last else ANY] + [VMEM] * 4,
        out_specs=[VMEM] * (4 + len(weights)),
        input_output_aliases={10: 0, 11: 1},
        scratch_shapes=[
            pltpu.VMEM((3, 8, BLOCK, LANES), F32),
            pltpu.VMEM((2 * LANES, width), BF16),
        ],
        compiler_params=params(),
        cost_estimate=SMALL,
        name=f"far{chunk}",
    )(lists, own2, rest2, *gos, after, earlier, state, kk, vv, qq)


def bwd_group(kk, vv, q2, g2, lse, delta, ks, vs, diag=None):
    scores = nt(q2, jnp.concatenate([kk[f] for f in ks], axis=0))
    dprob = nt(g2, jnp.concatenate([vv[f, :, 0:LANES] for f in ks], axis=0))
    probs, dscores = [], []
    for i in range(len(ks)):
        part = scores[:, i * BLOCK : (i + 1) * BLOCK]
        if diag == i:
            part = jnp.where(causal(part.shape), part, NEG)
        prob = jnp.exp(part - lse)
        dscores.append((prob * (dprob[:, i * BLOCK : (i + 1) * BLOCK] - delta)).astype(BF16))
        probs.append(prob)
    out = nn(jnp.concatenate(dscores, axis=1), jnp.concatenate([kk[f] for f in vs], axis=0))
    return probs, dscores, out


def back_kernel(chunk, which_d, list_ref, kk, vv, qq, g_ref, attn_ref, lse_ref, after, *refs):
    *outs, dq = refs
    r, _ = place()

    def query_side(qi):
        at = pl.ds(pl.multiple_of(qi * BLOCK, BLOCK), BLOCK)
        g = g_ref[at, chunk * LANES : (chunk + 1) * LANES]
        product = g.astype(F32) * attn_ref[at, :].astype(F32)
        low = low_lanes(product.shape)
        delta = jnp.concatenate(
            [
                jnp.sum(jnp.where(low, product, 0.0), axis=1, keepdims=True),
                jnp.sum(jnp.where(low, 0.0, product), axis=1, keepdims=True),
            ],
            axis=0,
        )
        half = LANES // 2
        lse = jnp.concatenate([lse_ref[qi, :, 0:1], lse_ref[qi, :, half : half + 1]], axis=0)
        return two_heads(qq[qi]), two_heads(g), lse, delta

    for n, d in enumerate(which_d):
        rho = r ^ d
        sides = [query_side(2 * rho + b) for b in (0, 1)]
        local = []
        for b in (0, 1):
            qi = 2 * rho + b
            ks, vs = slots_of(list_ref, qi, 0, list_ref[qi, COUNTS + 1], BACK_FIRST)
            own_ks, own_vs = own_slots(rho, b)
            probs, dscores, add = bwd_group(kk, vv, *sides[b], own_ks + ks, own_vs + vs, diag=1)
            dq[2 * n + b] = add
            local.append(([p.astype(BF16) for p in probs[:2]], dscores[:2]))
        out = outs[n]
        for which, side in ((1, 0), (0, 1)):
            both = jnp.concatenate([sides[0][side], sides[1][side]], axis=0)
            first = jnp.concatenate([local[0][which][1], local[1][which][0]], axis=0)
            base = 512 if side else 256
            out[base : base + BLOCK, :] = tn(first, both).astype(BF16)
            out[base + BLOCK : base + 256, :] = tn(local[1][which][1], sides[1][side]).astype(BF16)

    def overflow(n, carry):
        rho = r ^ ((n + which_d[0]) % ROW)
        counts = [list_ref[2 * rho + b, COUNTS + 1] for b in (0, 1)]

        def body(g, inner):
            for b in (0, 1):
                qi = 2 * rho + b
                ks, vs = slots_of(list_ref, qi, BACK_FIRST + 4 * g, counts[b], 4)
                _, _, add = bwd_group(kk, vv, *query_side(qi), ks, vs)
                dq[2 * n + b] += add
            return inner

        longest = jnp.maximum(counts[0], counts[1])
        return lax.fori_loop(0, (longest - BACK_FIRST + 3) // 4, body, carry)

    lax.fori_loop(0, len(which_d), overflow, 0)
    for n in range(len(which_d)):
        for b in (0, 1):
            outs[n][b * BLOCK : (b + 1) * BLOCK, :] = (pick(dq[2 * n + b]) * 0.125).astype(BF16)


def back(chunk, which_d, lists, kk, vv, qq, grads, attn, lse, after):
    return pl.pallas_call(
        functools.partial(back_kernel, chunk, which_d),
        out_shape=(jax.ShapeDtypeStruct((768, LANES), BF16),) * len(which_d),
        in_specs=[SMEM] + [VMEM] * 6 + [ANY],
        out_specs=[VMEM] * len(which_d),
        scratch_shapes=[pltpu.VMEM((2 * len(which_d), 2 * BLOCK, LANES), F32)],
        compiler_params=params(),
        cost_estimate=SMALL,
        name=f"back{chunk}_{which_d[0]}",
    )(lists, kk, vv, qq, grads, attn, lse, after)


def unpack_kernel(chunk, *refs):
    ins, outs = refs[:ROW], refs[-3:]
    r, _ = place()
    odd_me = (r % 2) == 1
    rows, width = outs[0].shape
    for pair in (0, 1):
        tile = (r // 2 + pair) % 2
        first, second = ins[2 * pair], ins[2 * pair + 1]
        for which, out in enumerate(outs):
            a = first[which * rows : (which + 1) * rows, :].astype(F32)
            b = second[which * rows : (which + 1) * rows, :].astype(F32)
            low, high = jnp.where(odd_me, b, a), jnp.where(odd_me, a, b)
            one, two = split_pair(low, high)
            out[:, pl.ds(pl.multiple_of(tile * LANES, LANES), LANES)] = one.astype(BF16)
            out[:, pl.ds(pl.multiple_of((tile + 2) * LANES, LANES), LANES)] = two.astype(BF16)


def unpack(chunk, pieces, rows, width, before):
    half = pl.BlockSpec((rows, width // 2), lambda i: (0, chunk))
    return pl.pallas_call(
        functools.partial(unpack_kernel, chunk),
        grid=(1,),
        out_shape=(jax.ShapeDtypeStruct((rows, width), BF16),) * 3,
        in_specs=[VMEM] * ROW + [ANY] * len(before),
        out_specs=[half] * 3,
        input_output_aliases={ROW + i: i for i in range(len(before))},
        compiler_params=params(),
        cost_estimate=SMALL,
        name=f"unpack{chunk}",
    )(*pieces, *before)


def swap(value, axis, bit):
    count = lax.axis_size(axis)
    return lax.ppermute(value, axis, [(s, s ^ bit) for s in range(count)])


def later(value, axis):
    count = lax.axis_size(axis)
    return lax.ppermute(value, axis, [(s, (s + ROW) % count) for s in range(count)])


hold = lax.optimization_barrier


def shards(queries, keys, values, track, out_weight, grad_out):
    rows, width = queries.shape
    count = lax.axis_size("span")
    fast = count == HEADS

    own0, firsts = pack_first(track, keys, values)
    own1 = later(own0, "span")
    got_first = [swap(x, "span", d + 1) for d, x in enumerate(firsts)]
    queries, _ = hold((queries, got_first[0]))
    seconds = list(pack_second(queries, keys, values))
    got_first, _ = hold((got_first, seconds[0]))
    rest0 = [stack(2 * rows, got_first)]
    rest1 = [later(rest0[0], "span")]
    track_row = jnp.concatenate(
        [track.astype(BF16)] + [x[2 * rows : 2 * rows + 2, : 2 * WINDOW] for x in got_first], axis=0
    )
    lists = plan(track_row.astype(jnp.int32))

    seconds, _ = hold((seconds, (rest0[0], own1)))
    seconds[1:] = [swap(seconds[d], "span", d) for d in (1, 2, 3)]
    own2 = later(own1, "span")
    arrived, _ = hold((seconds[1:], (rest1[0], own2, lists)))
    rest0.append(stack(2 * rows, arrived))
    rest1.append(later(rest0[1], "span"))
    grad_late, _ = hold((grad_out, rest0[1]))
    go2 = swap(grad_late, "span", 2)

    stores = [near(0, lists, own0, rest0[0], own1, rest1[0], seconds, lists)]
    first_row, _ = hold((rest1[0], stores[0][0]))
    rest2 = [later(first_row, "span"), later(rest1[1], "span")]
    (grad_late, go2), _ = hold(((grad_out, go2), (stores[0][0], rest1[1])))
    gos = (grad_out, swap(grad_late, "span", 1), go2, swap(go2, "span", 1))
    grads = grad_attn(out_weight, gos)
    stores.append(near(1, lists, own0, rest0[1], own1, rest1[1], seconds, stores[0][0]))

    after = stores[1][0]
    kk, vv, attn, lse, term = far(0, False, lists, own2, rest2[0], gos, after, after, *stores[0])
    out = back(0, (0, 1, 2, 3), lists, kk, vv, stores[0][3], grads, attn, lse, attn)
    pieces = [out[0]] + [swap(out[d], "span", d) for d in (1, 2, 3)]
    grads_out = unpack(0, pieces, rows, width, ())

    kk, vv, attn, lse, *terms = far(1, fast, lists, own2, rest2[1], gos, out[0], term, *stores[1])
    second = (lists, kk, vv, stores[1][3], grads, attn, lse)
    if fast:
        weight_grad = terms[0].astype(F32)
        for delta in (1, 2, 3):
            pairs = [
                (ROW * s + q, ROW * ((s + delta) % ROW) + q) for s in range(ROW) for q in range(ROW)
            ]
            weight_grad += lax.ppermute(terms[delta], "span", pairs).astype(F32)
    else:
        head_dim = width // HEADS
        place_in_row = lax.axis_index("span").astype(jnp.int32) % ROW
        mine = jnp.concatenate([term, terms[0]], axis=0).reshape(ROW, 1, head_dim, width)
        full = jnp.zeros((ROW, ROW, head_dim, width), BF16)
        full = lax.dynamic_update_slice(full, mine, (0, place_in_row, 0, 0)).reshape(width, width)
        weight_grad = lax.psum_scatter(full.astype(F32), "span", scatter_dimension=0, tiled=True)
    out = back(1, (1, 2, 3), *second, attn)
    out, grads_out = hold((out, grads_out))
    crossed = [swap(x, "span", d) for x, d in zip(out, (1, 2, 3))]
    (own,) = back(1, (0,), *second, out[0])
    pieces = [own] + crossed
    query_grad, key_grad, value_grad = unpack(1, pieces, rows, width, grads_out)
    return (query_grad, key_grad, value_grad, weight_grad)


def solution(mesh):
    spec = P(("groups", "span"), None)
    return jax.shard_map(
        shards,
        mesh=mesh,
        in_specs=(spec, spec, spec, spec, P(), spec),
        out_specs=(spec, spec, spec, spec),
        check_vma=False,
    )
```

```python
import functools

import jax
import jax.numpy as jnp
from jax import lax
from jax.experimental import pallas as pl
from jax.experimental.pallas import tpu as pltpu
from jax.sharding import PartitionSpec as P

HEADS = 16
BLOCK = 128
WINDOW = 8
ROW = 4
LANES = 128
NEG = -1e30
COUNTS = 24
SPARE, ZERO, SLOTS = 24, 28, 29
VMEM_LIMIT = 16 * 1024 * 1024
SMALL = pl.CostEstimate(flops=1_000_000, bytes_accessed=100_000, transcendentals=0)

F32 = jnp.float32
BF16 = jnp.bfloat16

ANY = pl.BlockSpec(memory_space=pl.ANY)
SMEM = pl.BlockSpec(memory_space=pltpu.SMEM)
VMEM = pl.BlockSpec(memory_space=pltpu.VMEM)


def nn(a, b):
    return lax.dot_general(a, b, (((1,), (0,)), ((), ())), preferred_element_type=F32)


def nt(a, b):
    return lax.dot_general(a, b, (((1,), (1,)), ((), ())), preferred_element_type=F32)


def tn(a, b):
    return lax.dot_general(a, b, (((0,), (0,)), ((), ())), preferred_element_type=F32)


def place():
    index = lax.axis_index("span").astype(jnp.int32)
    return index % ROW, index // ROW


def params():
    return pltpu.CompilerParams(vmem_limit_bytes=VMEM_LIMIT)


def micros(time):
    return pl.CostEstimate(flops=int(time * 1.1e9), bytes_accessed=100_000, transcendentals=0)


def split_pair(a, b):
    lane = lax.broadcasted_iota(jnp.int32, a.shape, 1)
    low = lane < LANES // 2
    even = jnp.where(low, a, pltpu.roll(b, LANES // 2, 1))
    odd = jnp.where(low, pltpu.roll(a, LANES // 2, 1), b)
    return even, odd


def packed(src, chunk, pair):
    r, _ = place()
    odd_me = (r % 2) == 1
    tile = 4 * chunk + (r // 2 + pair) % 2
    a = src[:, pl.ds(pl.multiple_of(tile * LANES, LANES), LANES)].astype(F32)
    b = src[:, pl.ds(pl.multiple_of((tile + 2) * LANES, LANES), LANES)].astype(F32)
    even, odd = split_pair(a, b)
    return jnp.where(odd_me, odd, even), jnp.where(odd_me, even, odd)


def pack_first_kernel(k_v, v_v, own_ref, o1, o2, o3):
    outs = (o1, o2, o3)
    rows = k_v.shape[0]
    for which, src in enumerate((k_v, v_v)):
        for side, value in enumerate(packed(src, 1, 0)):
            if side == 0:
                base = (2 + which) * rows
                own_ref[base : base + rows, :] = value.astype(BF16)
        for pair in (0, 1):
            for side, value in enumerate(packed(src, 0, pair)):
                d = 2 * pair + side
                value = value.astype(BF16)
                base = which * rows
                if d == 0:
                    own_ref[base : base + rows, :] = value
                else:
                    outs[d - 1][base : base + rows, :] = value


def pack_second_kernel(t_ref, q_ref, k_ref, v_ref, k1, k2, k3, *q_outs):
    rows = k_ref.shape[0]
    for out in (k1, k2, k3):
        out[2 * rows : 2 * rows + 16, :] = jnp.zeros((16, LANES), BF16)
        out[2 * rows : 2 * rows + t_ref.shape[0], 0 : t_ref.shape[1]] = t_ref[...].astype(F32).astype(BF16)
    for pair in (0, 1):
        for which, src in enumerate((k_ref, v_ref)):
            for side, value in enumerate(packed(src, 1, pair)):
                d = 2 * pair + side
                if d > 0:
                    (k1, k2, k3)[d - 1][which * rows : (which + 1) * rows, :] = value.astype(BF16)
        for chunk in (0, 1):
            for side, value in enumerate(packed(q_ref, chunk, pair)):
                q_outs[2 * pair + side][chunk * rows : (chunk + 1) * rows, :] = (value * 0.125).astype(BF16)


def pack_first(keys, values):
    rows = keys.shape[0]
    outs = pl.pallas_call(
        pack_first_kernel,
        out_shape=(jax.ShapeDtypeStruct((4 * rows, LANES), BF16),)
        + (jax.ShapeDtypeStruct((2 * rows, LANES), BF16),) * 3,
        in_specs=[VMEM] * 2,
        out_specs=[VMEM] * 4,
        compiler_params=params(),
        cost_estimate=SMALL,
        name="pack_first",
    )(keys, values)
    return outs[0], outs[1:]


def pack_second(track, queries, keys, values):
    rows = queries.shape[0]
    outs = pl.pallas_call(
        pack_second_kernel,
        out_shape=(jax.ShapeDtypeStruct((2 * rows + 16, LANES), BF16),) * 3
        + (jax.ShapeDtypeStruct((2 * rows, LANES), BF16),) * ROW,
        in_specs=[VMEM] * 4,
        out_specs=[VMEM] * (2 * ROW - 1),
        compiler_params=params(),
        cost_estimate=SMALL,
        name="pack_second",
    )(track, queries, keys, values)
    return outs[:3], list(outs[3:])


def stack_kernel(rows, a, b, c, out):
    for i, src in enumerate((a, b, c)):
        out[i * rows : (i + 1) * rows, :] = src[0:rows, :]


def stack(rows, pieces):
    return pl.pallas_call(
        functools.partial(stack_kernel, rows),
        out_shape=jax.ShapeDtypeStruct((3 * rows, LANES), BF16),
        in_specs=[VMEM] * 3,
        out_specs=VMEM,
        compiler_params=params(),
        cost_estimate=SMALL,
        name="stack",
    )(*pieces)


def grad_kernel(w, g0, g1, g2, g3, out, wide_w):
    r, _ = place()
    half = LANES // 2
    rows = g0.shape[0]
    for j in range(ROW):
        at = pl.multiple_of((ROW * j + r) * half, half)
        wide_w[j * half : (j + 1) * half, :] = w[pl.ds(at, half), :]
    for d, g in enumerate((g0, g1, g2, g3)):
        at = pl.multiple_of((r ^ d) * rows, rows)
        out[pl.ds(at, rows), :] = nt(g[...], wide_w[...]).astype(BF16)


def grad_attn(weight, gos):
    rows, width = gos[0].shape
    return pl.pallas_call(
        grad_kernel,
        out_shape=jax.ShapeDtypeStruct((ROW * rows, 2 * LANES), BF16),
        in_specs=[VMEM] * (1 + ROW),
        out_specs=VMEM,
        scratch_shapes=[pltpu.VMEM((2 * LANES, width), BF16)],
        compiler_params=params(),
        cost_estimate=SMALL,
        name="grad_attn",
    )(weight, *gos)


def plan_kernel(track_ref, list_ref):
    r, z = place()

    def one_query(qi, carry):
        rho = qi // 2
        span = ROW * z + rho
        source = 2 * (r ^ rho) + qi % 2

        near, total = jnp.int32(0), jnp.int32(0)
        for i in range(2 * WINDOW):
            u = span - (i // 2 + 1)
            use = jnp.logical_and(track_ref[source, i] == 1, u >= 0).astype(jnp.int32)
            safe = jnp.maximum(u, 0)
            back = z - safe // ROW
            list_ref[qi, total] = (back * ROW + safe % ROW) * 2 + i % 2
            near = near + jnp.where(back < 2, use, 0)
            total = total + use
        list_ref[qi, COUNTS] = near
        list_ref[qi, COUNTS + 1] = total
        return carry

    lax.fori_loop(0, 2 * ROW, one_query, 0)


def plan(track_row):
    return pl.pallas_call(
        plan_kernel,
        out_shape=jax.ShapeDtypeStruct((2 * ROW, COUNTS + 2), jnp.int32),
        in_specs=[SMEM],
        out_specs=SMEM,
        cost_estimate=SMALL,
        name="plan",
    )(track_row)


def low_lanes(shape):
    return lax.broadcasted_iota(jnp.int32, shape, 1) < LANES // 2


def two_heads(x):
    low, zero = low_lanes(x.shape), jnp.zeros_like(x)
    return jnp.concatenate([jnp.where(low, x, zero), jnp.where(low, zero, x)], axis=0)


def pick(x):
    return jnp.where(low_lanes((BLOCK, LANES)), x[:BLOCK], x[BLOCK:])


def causal(shape):
    query = lax.broadcasted_iota(jnp.int32, shape, 0) % BLOCK
    return lax.broadcasted_iota(jnp.int32, shape, 1) <= query


def gather_row(r, chunk, back, own, rest, kk, vv):
    for d in range(ROW):
        src, base = (own, 512 * chunk) if d == 0 else (rest, 512 * (d - 1))
        for b in (0, 1):
            f = 8 * back + 2 * (r ^ d) + b
            at = base + b * BLOCK
            kk[f] = src[at : at + BLOCK, :]
            vv[f, :, 0:LANES] = src[at + 256 : at + 256 + BLOCK, :]


def gather_queries(r, chunk, seconds, qq):
    for d, second in enumerate(seconds):
        for b in (0, 1):
            at = chunk * 256 + b * BLOCK
            qq[2 * (r ^ d) + b] = second[at : at + BLOCK, :]


def slots_of(list_ref, qi, start, count, how_many):
    ks, vs = [], []
    for i in range(how_many):
        position = start + i
        inside = position < count
        f = list_ref[qi, jnp.minimum(position, COUNTS - 1)]
        ks.append(jnp.where(inside, f, SPARE + qi // 2))
        vs.append(jnp.where(inside, f, ZERO))
    return ks, vs


def own_slots(rho, b):
    return [2 * rho if b else SPARE + rho, 2 * rho + b], [2 * rho if b else ZERO, 2 * rho + b]


def fwd_group(kk, vv, q2, ks, vs, diag=None):
    scores = nt(q2, jnp.concatenate([kk[f] for f in ks], axis=0))
    parts = [scores[:, i * BLOCK : (i + 1) * BLOCK] for i in range(len(ks))]
    if diag is not None:
        parts[diag] = jnp.where(causal(parts[diag].shape), parts[diag], NEG)
    top = jnp.max(functools.reduce(jnp.maximum, parts), axis=1, keepdims=True)
    expo = jnp.concatenate([jnp.exp(part - top).astype(BF16) for part in parts], axis=1)
    out = nn(expo, jnp.concatenate([vv[f] for f in vs], axis=0))
    return pick(jnp.broadcast_to(top, (2 * BLOCK, LANES))), pick(out[:, LANES:]), pick(out[:, :LANES])


def merge(before, state, qi, group):
    m, l, num = before[0, qi], before[1, qi], before[2, qi]
    top = jnp.maximum(m, group[0])
    old, new = jnp.exp(m - top), jnp.exp(group[0] - top)
    state[0, qi] = top
    state[1, qi] = l * old + group[1] * new
    state[2, qi] = num * old + group[2] * new


NEAR_FIRST = tuple(6 + 2 * (rho // 2) for rho in range(ROW))
FAR_FIRST = tuple(6 - 2 * ((rho + 1) // 2) for rho in range(ROW))
BACK_FIRST = 10


def near_kernel(
    chunk, list_ref, own0, rest0, own1, rest1, s0, s1, s2, s3, after, state, kk, vv, qq
):
    r, _ = place()
    gather_row(r, chunk, 0, own0, rest0, kk, vv)
    gather_row(r, chunk, 1, own1, rest1, kk, vv)
    gather_queries(r, chunk, (s0, s1, s2, s3), qq)
    kk[ZERO] = jnp.zeros((BLOCK, LANES), BF16)
    for f in range(SLOTS):
        if f < SPARE:
            vv[f, :, LANES : 2 * LANES] = jnp.ones((BLOCK, LANES), BF16)
        else:
            vv[f] = jnp.zeros((BLOCK, 2 * LANES), BF16)
    for rho in range(ROW):
        kk[SPARE + rho] = jnp.broadcast_to(kk[2 * rho, 0:1, :], (BLOCK, LANES))
    for qi in range(2 * ROW):
        rho, b = qi // 2, qi % 2
        ks, vs = slots_of(list_ref, qi, 0, list_ref[qi, COUNTS], NEAR_FIRST[rho])
        own_ks, own_vs = own_slots(rho, b)
        group = fwd_group(kk, vv, two_heads(qq[qi]), own_ks + ks, own_vs + vs, diag=1)
        for i, value in enumerate(group):
            state[i, qi] = value

    def overflow(rho, carry):
        first = NEAR_FIRST[0] + 2 * (rho // 2)
        counts = [list_ref[2 * rho + b, COUNTS] for b in (0, 1)]

        def body(g, inner):
            for b in (0, 1):
                qi = 2 * rho + b
                ks, vs = slots_of(list_ref, qi, first + 4 * g, counts[b], 4)
                merge(state, state, qi, fwd_group(kk, vv, two_heads(qq[qi]), ks, vs))
            return inner

        return lax.fori_loop(0, (jnp.maximum(counts[0], counts[1]) - first + 3) // 4, body, carry)

    lax.fori_loop(0, ROW, overflow, 0)


def near(chunk, lists, own0, rest0, own1, rest1, seconds, after):
    return pl.pallas_call(
        functools.partial(near_kernel, chunk),
        out_shape=(
            jax.ShapeDtypeStruct((3, 8, BLOCK, LANES), F32),
            jax.ShapeDtypeStruct((SLOTS, BLOCK, LANES), BF16),
            jax.ShapeDtypeStruct((SLOTS, BLOCK, 2 * LANES), BF16),
            jax.ShapeDtypeStruct((8, BLOCK, LANES), BF16),
        ),
        in_specs=[SMEM] + [VMEM] * 8 + [ANY],
        out_specs=[VMEM] * 4,
        compiler_params=params(),
        cost_estimate=SMALL if chunk else micros(5.5),
        name=f"near{chunk}",
    )(lists, own0, rest0, own1, rest1, *seconds, after)


def far_kernel(
    chunk, last, list_ref, own2, rest2, after, state_in, kk_in, vv_in, qq, *refs
):
    if last:
        earlier, *gos = refs[: 1 + ROW]
        refs = refs[1 + ROW :]
    kk, vv, attn_ref, lse_ref, *terms, state, wide = refs
    r, z = place()
    gather_row(r, chunk, 2, own2, rest2, kk, vv)
    for qi in range(2 * ROW):
        ks, vs = slots_of(
            list_ref, qi, list_ref[qi, COUNTS], list_ref[qi, COUNTS + 1], FAR_FIRST[qi // 2]
        )
        group = fwd_group(kk, vv, two_heads(qq[qi]), ks, vs)
        merge(state_in, state, qi, group)

    def overflow(rho, carry):
        first = FAR_FIRST[0] - 2 * ((rho + 1) // 2)
        starts = [list_ref[2 * rho + b, COUNTS] + first for b in (0, 1)]
        counts = [list_ref[2 * rho + b, COUNTS + 1] for b in (0, 1)]

        def body(g, inner):
            for b in (0, 1):
                qi = 2 * rho + b
                ks, vs = slots_of(list_ref, qi, starts[b] + 4 * g, counts[b], 4)
                merge(state, state, qi, fwd_group(kk, vv, two_heads(qq[qi]), ks, vs))
            return inner

        longest = jnp.maximum(counts[0] - starts[0], counts[1] - starts[1])
        return lax.fori_loop(0, (longest + 3) // 4, body, carry)

    lax.fori_loop(0, ROW, overflow, 0)
    for qi in range(2 * ROW):
        lse_ref[qi] = state[0, qi] + jnp.log(state[1, qi])
        attn_ref[qi * BLOCK : (qi + 1) * BLOCK, :] = (state[2, qi] / state[1, qi]).astype(BF16)
    if not last:
        return
    total = None
    for d, g in enumerate(gos):
        rows = g.shape[0]
        at = pl.ds(pl.multiple_of((r ^ d) * rows, rows), rows)
        part = tn(jnp.concatenate([earlier[at, :], attn_ref[at, :]], axis=1), g[...])
        total = part if total is None else total + part
    if len(terms) == 1:
        terms[0][...] = total.astype(BF16)
        return
    wide[...] = total.astype(BF16)
    half = LANES // 2
    for delta, out in enumerate(terms):
        at = pl.multiple_of((z + delta) % ROW * half, half)
        out[...] = wide[pl.ds(at, half), :]


def far(chunk, fast, lists, own2, rest2, after, state, kk, vv, qq, earlier=None, gos=()):
    last = len(gos) > 0
    width = gos[0].shape[1] if last else LANES
    weights = (jax.ShapeDtypeStruct((LANES // 2, width), BF16),) * ROW
    if not fast:
        weights = (jax.ShapeDtypeStruct((2 * LANES, width), BF16),)
    if not last:
        weights = ()
    more = (earlier, *gos) if last else ()
    return pl.pallas_call(
        functools.partial(far_kernel, chunk, last),
        out_shape=(
            jax.ShapeDtypeStruct(kk.shape, BF16),
            jax.ShapeDtypeStruct(vv.shape, BF16),
            jax.ShapeDtypeStruct((8 * BLOCK, LANES), BF16),
            jax.ShapeDtypeStruct((8, BLOCK, LANES), F32),
        )
        + weights,
        in_specs=[SMEM] + [VMEM] * 2 + [ANY] + [VMEM] * (4 + len(more)),
        out_specs=[VMEM] * (4 + len(weights)),
        input_output_aliases={5: 0, 6: 1},
        scratch_shapes=[
            pltpu.VMEM((3, 8, BLOCK, LANES), F32),
            pltpu.VMEM((2 * LANES, width), BF16),
        ],
        compiler_params=params(),
        cost_estimate=SMALL if last else micros(4.2),
        name=f"far{chunk}",
    )(lists, own2, rest2, after, state, kk, vv, qq, *more)


def bwd_group(kk, vv, q2, g2, lse, delta, ks, vs, diag=None):
    scores = nt(q2, jnp.concatenate([kk[f] for f in ks], axis=0))
    dprob = nt(g2, jnp.concatenate([vv[f, :, 0:LANES] for f in ks], axis=0))
    probs, dscores = [], []
    for i in range(len(ks)):
        part = scores[:, i * BLOCK : (i + 1) * BLOCK]
        if diag == i:
            part = jnp.where(causal(part.shape), part, NEG)
        prob = jnp.exp(part - lse)
        dscores.append((prob * (dprob[:, i * BLOCK : (i + 1) * BLOCK] - delta)).astype(BF16))
        probs.append(prob)
    out = nn(jnp.concatenate(dscores, axis=1), jnp.concatenate([kk[f] for f in vs], axis=0))
    return probs, dscores, out


def back_kernel(chunk, which_d, list_ref, kk, vv, qq, g_ref, attn_ref, lse_ref, after, *refs):
    *outs, dq = refs
    r, _ = place()

    def query_side(qi):
        at = pl.ds(pl.multiple_of(qi * BLOCK, BLOCK), BLOCK)
        g = g_ref[at, chunk * LANES : (chunk + 1) * LANES]
        product = g.astype(F32) * attn_ref[at, :].astype(F32)
        low = low_lanes(product.shape)
        delta = jnp.concatenate(
            [
                jnp.sum(jnp.where(low, product, 0.0), axis=1, keepdims=True),
                jnp.sum(jnp.where(low, 0.0, product), axis=1, keepdims=True),
            ],
            axis=0,
        )
        half = LANES // 2
        lse = jnp.concatenate([lse_ref[qi, :, 0:1], lse_ref[qi, :, half : half + 1]], axis=0)
        return two_heads(qq[qi]), two_heads(g), lse, delta

    for n, d in enumerate(which_d):
        rho = r ^ d
        sides = [query_side(2 * rho + b) for b in (0, 1)]
        local = []
        for b in (0, 1):
            qi = 2 * rho + b
            ks, vs = slots_of(list_ref, qi, 0, list_ref[qi, COUNTS + 1], BACK_FIRST)
            own_ks, own_vs = own_slots(rho, b)
            probs, dscores, add = bwd_group(kk, vv, *sides[b], own_ks + ks, own_vs + vs, diag=1)
            dq[2 * n + b] = add
            local.append(([p.astype(BF16) for p in probs[:2]], dscores[:2]))
        out = outs[n]
        for which, side in ((1, 0), (0, 1)):
            both = jnp.concatenate([sides[0][side], sides[1][side]], axis=0)
            first = jnp.concatenate([local[0][which][1], local[1][which][0]], axis=0)
            base = 512 if side else 256
            out[base : base + BLOCK, :] = tn(first, both).astype(BF16)
            out[base + BLOCK : base + 256, :] = tn(local[1][which][1], sides[1][side]).astype(BF16)

    def overflow(n, carry):
        rho = r ^ ((n + which_d[0]) % ROW)
        counts = [list_ref[2 * rho + b, COUNTS + 1] for b in (0, 1)]

        def body(g, inner):
            for b in (0, 1):
                qi = 2 * rho + b
                ks, vs = slots_of(list_ref, qi, BACK_FIRST + 4 * g, counts[b], 4)
                _, _, add = bwd_group(kk, vv, *query_side(qi), ks, vs)
                dq[2 * n + b] += add
            return inner

        longest = jnp.maximum(counts[0], counts[1])
        return lax.fori_loop(0, (longest - BACK_FIRST + 3) // 4, body, carry)

    lax.fori_loop(0, len(which_d), overflow, 0)
    for n in range(len(which_d)):
        for b in (0, 1):
            outs[n][b * BLOCK : (b + 1) * BLOCK, :] = (pick(dq[2 * n + b]) * 0.125).astype(BF16)


def back(chunk, which_d, lists, kk, vv, qq, grads, attn, lse, after):
    return pl.pallas_call(
        functools.partial(back_kernel, chunk, which_d),
        out_shape=(jax.ShapeDtypeStruct((768, LANES), BF16),) * len(which_d),
        in_specs=[SMEM] + [VMEM] * 6 + [ANY],
        out_specs=[VMEM] * len(which_d),
        scratch_shapes=[pltpu.VMEM((2 * len(which_d), 2 * BLOCK, LANES), F32)],
        compiler_params=params(),
        cost_estimate=SMALL if chunk else micros(8.4),
        name=f"back{chunk}_{which_d[0]}",
    )(lists, kk, vv, qq, grads, attn, lse, after)


def unpack_kernel(chunk, *refs):
    ins, outs = refs[:ROW], refs[-3:]
    r, _ = place()
    odd_me = (r % 2) == 1
    rows, width = outs[0].shape
    for pair in (0, 1):
        tile = (r // 2 + pair) % 2
        first, second = ins[2 * pair], ins[2 * pair + 1]
        for which, out in enumerate(outs):
            a = first[which * rows : (which + 1) * rows, :].astype(F32)
            b = second[which * rows : (which + 1) * rows, :].astype(F32)
            low, high = jnp.where(odd_me, b, a), jnp.where(odd_me, a, b)
            one, two = split_pair(low, high)
            out[:, pl.ds(pl.multiple_of(tile * LANES, LANES), LANES)] = one.astype(BF16)
            out[:, pl.ds(pl.multiple_of((tile + 2) * LANES, LANES), LANES)] = two.astype(BF16)


def unpack(chunk, pieces, rows, width, before):
    half = pl.BlockSpec((rows, width // 2), lambda i: (0, chunk))
    return pl.pallas_call(
        functools.partial(unpack_kernel, chunk),
        grid=(1,),
        out_shape=(jax.ShapeDtypeStruct((rows, width), BF16),) * 3,
        in_specs=[VMEM] * ROW + [ANY] * len(before),
        out_specs=[half] * 3,
        input_output_aliases={ROW + i: i for i in range(len(before))},
        compiler_params=params(),
        cost_estimate=SMALL,
        name=f"unpack{chunk}",
    )(*pieces, *before)


def swap(value, axis, bit):
    count = lax.axis_size(axis)
    return lax.ppermute(value, axis, [(s, s ^ bit) for s in range(count)])


def later(value, axis):
    count = lax.axis_size(axis)
    return lax.ppermute(value, axis, [(s, (s + ROW) % count) for s in range(count)])


hold = lax.optimization_barrier


def shards(queries, keys, values, track, out_weight, grad_out):
    rows, width = queries.shape
    count = lax.axis_size("span")
    fast = count == HEADS

    own0, firsts = pack_first(keys, values)
    own1 = later(own0, "span")
    got_first = [swap(x, "span", d + 1) for d, x in enumerate(firsts)]
    queries, _ = hold((queries, got_first[0]))
    seconds, turns = pack_second(track, queries, keys, values)
    got_first, _ = hold((got_first, seconds[0]))
    rest0 = [stack(2 * rows, got_first)]
    rest1 = [later(rest0[0], "span")]
    seconds, _ = hold((seconds, (rest0[0], own1)))
    got_second = [swap(x, "span", d + 1) for d, x in enumerate(seconds)]
    track_row = jnp.concatenate(
        [track.astype(BF16)] + [x[2 * rows : 2 * rows + 2, : 2 * WINDOW] for x in got_second], axis=0
    )
    lists = plan(track_row.astype(jnp.int32))

    got_second, _ = hold((got_second, rest1[0]))
    rest0.append(stack(2 * rows, got_second))
    turns, _ = hold((turns, (rest0[1], rest1[0])))
    rest1.append(later(rest0[1], "span"))
    own1_late, _ = hold((own1, rest1[1]))
    own2 = later(own1_late, "span")
    turns[1:] = [swap(turns[d], "span", d) for d in (1, 2, 3)]
    grad_late, _ = hold((grad_out, (turns, rest1[1])))
    go2 = swap(grad_late, "span", 2)

    turns, _ = hold((turns, rest1[1]))
    stores = [near(0, lists, own0, rest0[0], own1, rest1[0], turns, lists)]
    stores.append(near(1, lists, own0, rest0[1], own1, rest1[1], turns, stores[0][0]))
    first_row, _ = hold((rest1[0], rest1[1]))
    (second_row, grad_late, go2), _ = hold(((rest1[1], grad_out, go2), stores[1][0]))
    rest2 = [later(first_row, "span"), later(second_row, "span")]
    gos = (grad_out, swap(grad_late, "span", 1), go2, swap(go2, "span", 1))
    grads = grad_attn(out_weight, gos)

    after = stores[1][0]
    kk, vv, attn, lse = far(0, fast, lists, own2, rest2[0], after, *stores[0])
    out = back(0, (0, 1, 2, 3), lists, kk, vv, stores[0][3], grads, attn, lse, attn)
    pieces = [out[0]] + [swap(out[d], "span", d) for d in (1, 2, 3)]

    kk, vv, attn, lse, *terms = far(
        1, fast, lists, own2, rest2[1], out[0], *stores[1], earlier=attn, gos=gos
    )
    second = (lists, kk, vv, stores[1][3], grads, attn, lse)
    if fast:
        weight_grad = terms[0].astype(F32)
        for delta in (1, 2, 3):
            pairs = [
                (ROW * s + q, ROW * ((s + delta) % ROW) + q) for s in range(ROW) for q in range(ROW)
            ]
            weight_grad += lax.ppermute(terms[delta], "span", pairs).astype(F32)
    else:
        head_dim = width // HEADS
        place_in_row = lax.axis_index("span").astype(jnp.int32) % ROW
        mine = terms[0].reshape(ROW, 1, head_dim, width)
        full = jnp.zeros((ROW, ROW, head_dim, width), BF16)
        full = lax.dynamic_update_slice(full, mine, (0, place_in_row, 0, 0)).reshape(width, width)
        weight_grad = lax.psum_scatter(full.astype(F32), "span", scatter_dimension=0, tiled=True)
    out = back(1, (1, 2, 3), *second, attn)
    out, pieces = hold((out, pieces))
    grads_out = unpack(0, pieces, rows, width, ())
    crossed = [swap(x, "span", d) for x, d in zip(out, (1, 2, 3))]
    (own,) = back(1, (0,), *second, out[0])
    pieces = [own] + crossed
    query_grad, key_grad, value_grad = unpack(1, pieces, rows, width, grads_out)
    return (query_grad, key_grad, value_grad, weight_grad)


def solution(mesh):
    spec = P(("groups", "span"), None)
    return jax.shard_map(
        shards,
        mesh=mesh,
        in_specs=(spec, spec, spec, spec, P(), spec),
        out_specs=(spec, spec, spec, spec),
        check_vma=False,
    )
```

```python
import functools

import jax
import jax.numpy as jnp
from jax import lax
from jax.experimental import pallas as pl
from jax.experimental.pallas import tpu as pltpu
from jax.sharding import PartitionSpec as P

HEADS = 16
BLOCK = 128
WINDOW = 8
ROW = 4
LANES = 128
NEG = -1e30
COUNTS = 24
SPARE, ZERO, SLOTS = 24, 28, 29
VMEM_LIMIT = 16 * 1024 * 1024
SMALL = pl.CostEstimate(flops=1_000_000, bytes_accessed=100_000, transcendentals=0)

F32 = jnp.float32
BF16 = jnp.bfloat16

ANY = pl.BlockSpec(memory_space=pl.ANY)
SMEM = pl.BlockSpec(memory_space=pltpu.SMEM)
VMEM = pl.BlockSpec(memory_space=pltpu.VMEM)


def nn(a, b):
    return lax.dot_general(a, b, (((1,), (0,)), ((), ())), preferred_element_type=F32)


def nt(a, b):
    return lax.dot_general(a, b, (((1,), (1,)), ((), ())), preferred_element_type=F32)


def tn(a, b):
    return lax.dot_general(a, b, (((0,), (0,)), ((), ())), preferred_element_type=F32)


def place():
    index = lax.axis_index("span").astype(jnp.int32)
    return index % ROW, index // ROW


def params():
    return pltpu.CompilerParams(vmem_limit_bytes=VMEM_LIMIT)


def micros(time):
    return pl.CostEstimate(flops=int(time * 1.1e9), bytes_accessed=100_000, transcendentals=0)


def split_pair(a, b):
    lane = lax.broadcasted_iota(jnp.int32, a.shape, 1)
    low = lane < LANES // 2
    even = jnp.where(low, a, pltpu.roll(b, LANES // 2, 1))
    odd = jnp.where(low, pltpu.roll(a, LANES // 2, 1), b)
    return even, odd


def packed(src, chunk, pair):
    r, _ = place()
    odd_me = (r % 2) == 1
    tile = 4 * chunk + (r // 2 + pair) % 2
    a = src[:, pl.ds(pl.multiple_of(tile * LANES, LANES), LANES)].astype(F32)
    b = src[:, pl.ds(pl.multiple_of((tile + 2) * LANES, LANES), LANES)].astype(F32)
    even, odd = split_pair(a, b)
    return jnp.where(odd_me, odd, even), jnp.where(odd_me, even, odd)


def pack_first_kernel(k_v, v_v, own_ref, o1, o2, o3):
    outs = (o1, o2, o3)
    rows = k_v.shape[0]
    for which, src in enumerate((k_v, v_v)):
        for side, value in enumerate(packed(src, 1, 0)):
            if side == 0:
                base = (2 + which) * rows
                own_ref[base : base + rows, :] = value.astype(BF16)
        for pair in (0, 1):
            for side, value in enumerate(packed(src, 0, pair)):
                d = 2 * pair + side
                value = value.astype(BF16)
                base = which * rows
                if d == 0:
                    own_ref[base : base + rows, :] = value
                else:
                    outs[d - 1][base : base + rows, :] = value


def pack_second_kernel(t_ref, q_ref, k_ref, v_ref, k1, k2, k3, *q_outs):
    rows = k_ref.shape[0]
    for out in (k1, k2, k3):
        out[2 * rows : 2 * rows + 16, :] = jnp.zeros((16, LANES), BF16)
        out[2 * rows : 2 * rows + t_ref.shape[0], 0 : t_ref.shape[1]] = t_ref[...].astype(F32).astype(BF16)
    for pair in (0, 1):
        for which, src in enumerate((k_ref, v_ref)):
            for side, value in enumerate(packed(src, 1, pair)):
                d = 2 * pair + side
                if d > 0:
                    (k1, k2, k3)[d - 1][which * rows : (which + 1) * rows, :] = value.astype(BF16)
        for chunk in (0, 1):
            for side, value in enumerate(packed(q_ref, chunk, pair)):
                q_outs[2 * pair + side][chunk * rows : (chunk + 1) * rows, :] = (value * 0.125).astype(BF16)


def pack_first(keys, values):
    rows = keys.shape[0]
    outs = pl.pallas_call(
        pack_first_kernel,
        out_shape=(jax.ShapeDtypeStruct((4 * rows, LANES), BF16),)
        + (jax.ShapeDtypeStruct((2 * rows, LANES), BF16),) * 3,
        in_specs=[VMEM] * 2,
        out_specs=[VMEM] * 4,
        compiler_params=params(),
        cost_estimate=SMALL,
        name="pack_first",
    )(keys, values)
    return outs[0], outs[1:]


def pack_second(track, queries, keys, values):
    rows = queries.shape[0]
    outs = pl.pallas_call(
        pack_second_kernel,
        out_shape=(jax.ShapeDtypeStruct((2 * rows + 16, LANES), BF16),) * 3
        + (jax.ShapeDtypeStruct((2 * rows, LANES), BF16),) * ROW,
        in_specs=[VMEM] * 4,
        out_specs=[VMEM] * (2 * ROW - 1),
        compiler_params=params(),
        cost_estimate=SMALL,
        name="pack_second",
    )(track, queries, keys, values)
    return outs[:3], list(outs[3:])


def stack_kernel(rows, a, b, c, out):
    for i, src in enumerate((a, b, c)):
        out[i * rows : (i + 1) * rows, :] = src[0:rows, :]


def stack(rows, pieces):
    return pl.pallas_call(
        functools.partial(stack_kernel, rows),
        out_shape=jax.ShapeDtypeStruct((3 * rows, LANES), BF16),
        in_specs=[VMEM] * 3,
        out_specs=VMEM,
        compiler_params=params(),
        cost_estimate=SMALL,
        name="stack",
    )(*pieces)


def grad_kernel(w, g0, g1, g2, g3, out, wide_w):
    r, _ = place()
    half = LANES // 2
    rows = g0.shape[0]
    for j in range(ROW):
        at = pl.multiple_of((ROW * j + r) * half, half)
        wide_w[j * half : (j + 1) * half, :] = w[pl.ds(at, half), :]
    for d, g in enumerate((g0, g1, g2, g3)):
        at = pl.multiple_of((r ^ d) * rows, rows)
        out[pl.ds(at, rows), :] = nt(g[...], wide_w[...]).astype(BF16)


def grad_attn(weight, gos):
    rows, width = gos[0].shape
    return pl.pallas_call(
        grad_kernel,
        out_shape=jax.ShapeDtypeStruct((ROW * rows, 2 * LANES), BF16),
        in_specs=[VMEM] * (1 + ROW),
        out_specs=VMEM,
        scratch_shapes=[pltpu.VMEM((2 * LANES, width), BF16)],
        compiler_params=params(),
        cost_estimate=SMALL,
        name="grad_attn",
    )(weight, *gos)


def plan_kernel(track_ref, list_ref):
    r, z = place()

    def one_query(qi, carry):
        rho = qi // 2
        span = ROW * z + rho
        source = 2 * (r ^ rho) + qi % 2

        near, total = jnp.int32(0), jnp.int32(0)
        for i in range(2 * WINDOW):
            u = span - (i // 2 + 1)
            use = jnp.logical_and(track_ref[source, i] == 1, u >= 0).astype(jnp.int32)
            safe = jnp.maximum(u, 0)
            back = z - safe // ROW
            list_ref[qi, total] = (back * ROW + safe % ROW) * 2 + i % 2
            near = near + jnp.where(back < 2, use, 0)
            total = total + use
        list_ref[qi, COUNTS] = near
        list_ref[qi, COUNTS + 1] = total
        return carry

    lax.fori_loop(0, 2 * ROW, one_query, 0)


def plan(track_row):
    return pl.pallas_call(
        plan_kernel,
        out_shape=jax.ShapeDtypeStruct((2 * ROW, COUNTS + 2), jnp.int32),
        in_specs=[SMEM],
        out_specs=SMEM,
        cost_estimate=SMALL,
        name="plan",
    )(track_row)


def low_lanes(shape):
    return lax.broadcasted_iota(jnp.int32, shape, 1) < LANES // 2


def two_heads(x):
    low, zero = low_lanes(x.shape), jnp.zeros_like(x)
    return jnp.concatenate([jnp.where(low, x, zero), jnp.where(low, zero, x)], axis=0)


def pick(x):
    return jnp.where(low_lanes((BLOCK, LANES)), x[:BLOCK], x[BLOCK:])


def causal(shape):
    query = lax.broadcasted_iota(jnp.int32, shape, 0) % BLOCK
    return lax.broadcasted_iota(jnp.int32, shape, 1) <= query


def gather_row(r, chunk, back, own, rest, kk, vv):
    for d in range(ROW):
        src, base = (own, 512 * chunk) if d == 0 else (rest, 512 * (d - 1))
        for b in (0, 1):
            f = 8 * back + 2 * (r ^ d) + b
            at = base + b * BLOCK
            kk[f] = src[at : at + BLOCK, :]
            vv[f, :, 0:LANES] = src[at + 256 : at + 256 + BLOCK, :]


def gather_queries(r, chunk, seconds, qq):
    for d, second in enumerate(seconds):
        for b in (0, 1):
            at = chunk * 256 + b * BLOCK
            qq[2 * (r ^ d) + b] = second[at : at + BLOCK, :]


def slots_of(list_ref, qi, start, count, how_many):
    ks, vs = [], []
    for i in range(how_many):
        position = start + i
        inside = position < count
        f = list_ref[qi, jnp.minimum(position, COUNTS - 1)]
        ks.append(jnp.where(inside, f, SPARE + qi // 2))
        vs.append(jnp.where(inside, f, ZERO))
    return ks, vs


def own_slots(rho, b):
    return [2 * rho if b else SPARE + rho, 2 * rho + b], [2 * rho if b else ZERO, 2 * rho + b]


def fwd_group(kk, vv, q2, ks, vs, diag=None):
    scores = nt(q2, jnp.concatenate([kk[f] for f in ks], axis=0))
    parts = [scores[:, i * BLOCK : (i + 1) * BLOCK] for i in range(len(ks))]
    if diag is not None:
        parts[diag] = jnp.where(causal(parts[diag].shape), parts[diag], NEG)
    top = jnp.max(functools.reduce(jnp.maximum, parts), axis=1, keepdims=True)
    expo = jnp.concatenate([jnp.exp(part - top).astype(BF16) for part in parts], axis=1)
    out = nn(expo, jnp.concatenate([vv[f] for f in vs], axis=0))
    return pick(jnp.broadcast_to(top, (2 * BLOCK, LANES))), pick(out[:, LANES:]), pick(out[:, :LANES])


def merge(before, state, qi, group):
    m, l, num = before[0, qi], before[1, qi], before[2, qi]
    top = jnp.maximum(m, group[0])
    old, new = jnp.exp(m - top), jnp.exp(group[0] - top)
    state[0, qi] = top
    state[1, qi] = l * old + group[1] * new
    state[2, qi] = num * old + group[2] * new


NEAR_FIRST = tuple(6 + 2 * (rho // 2) for rho in range(ROW))
FAR_FIRST = tuple(6 - 2 * ((rho + 1) // 2) for rho in range(ROW))
BACK_FIRST = 10


def near_kernel(
    chunk, list_ref, own0, rest0, own1, rest1, s0, s1, s2, s3, after, state, kk, vv, qq
):
    r, _ = place()
    gather_row(r, chunk, 0, own0, rest0, kk, vv)
    gather_row(r, chunk, 1, own1, rest1, kk, vv)
    gather_queries(r, chunk, (s0, s1, s2, s3), qq)
    kk[ZERO] = jnp.zeros((BLOCK, LANES), BF16)
    for f in range(SLOTS):
        if f < SPARE:
            vv[f, :, LANES : 2 * LANES] = jnp.ones((BLOCK, LANES), BF16)
        else:
            vv[f] = jnp.zeros((BLOCK, 2 * LANES), BF16)
    for rho in range(ROW):
        kk[SPARE + rho] = jnp.broadcast_to(kk[2 * rho, 0:1, :], (BLOCK, LANES))
    for qi in range(2 * ROW):
        rho, b = qi // 2, qi % 2
        ks, vs = slots_of(list_ref, qi, 0, list_ref[qi, COUNTS], NEAR_FIRST[rho])
        own_ks, own_vs = own_slots(rho, b)
        group = fwd_group(kk, vv, two_heads(qq[qi]), own_ks + ks, own_vs + vs, diag=1)
        for i, value in enumerate(group):
            state[i, qi] = value

    def overflow(rho, carry):
        first = NEAR_FIRST[0] + 2 * (rho // 2)
        counts = [list_ref[2 * rho + b, COUNTS] for b in (0, 1)]

        def body(g, inner):
            for b in (0, 1):
                qi = 2 * rho + b
                ks, vs = slots_of(list_ref, qi, first + 4 * g, counts[b], 4)
                merge(state, state, qi, fwd_group(kk, vv, two_heads(qq[qi]), ks, vs))
            return inner

        return lax.fori_loop(0, (jnp.maximum(counts[0], counts[1]) - first + 3) // 4, body, carry)

    lax.fori_loop(0, ROW, overflow, 0)


def near(chunk, lists, own0, rest0, own1, rest1, seconds, after):
    return pl.pallas_call(
        functools.partial(near_kernel, chunk),
        out_shape=(
            jax.ShapeDtypeStruct((3, 8, BLOCK, LANES), F32),
            jax.ShapeDtypeStruct((SLOTS, BLOCK, LANES), BF16),
            jax.ShapeDtypeStruct((SLOTS, BLOCK, 2 * LANES), BF16),
            jax.ShapeDtypeStruct((8, BLOCK, LANES), BF16),
        ),
        in_specs=[SMEM] + [VMEM] * 8 + [ANY],
        out_specs=[VMEM] * 4,
        compiler_params=params(),
        cost_estimate=SMALL if chunk else micros(5.5),
        name=f"near{chunk}",
    )(lists, own0, rest0, own1, rest1, *seconds, after)


def far_kernel(
    chunk, last, list_ref, own2, rest2, after, state_in, kk_in, vv_in, qq, *refs
):
    if last:
        earlier, *gos = refs[: 1 + ROW]
        refs = refs[1 + ROW :]
    kk, vv, attn_ref, lse_ref, *terms, state, wide = refs
    r, z = place()
    gather_row(r, chunk, 2, own2, rest2, kk, vv)
    for qi in range(2 * ROW):
        ks, vs = slots_of(
            list_ref, qi, list_ref[qi, COUNTS], list_ref[qi, COUNTS + 1], FAR_FIRST[qi // 2]
        )
        group = fwd_group(kk, vv, two_heads(qq[qi]), ks, vs)
        merge(state_in, state, qi, group)

    def overflow(rho, carry):
        first = FAR_FIRST[0] - 2 * ((rho + 1) // 2)
        starts = [list_ref[2 * rho + b, COUNTS] + first for b in (0, 1)]
        counts = [list_ref[2 * rho + b, COUNTS + 1] for b in (0, 1)]

        def body(g, inner):
            for b in (0, 1):
                qi = 2 * rho + b
                ks, vs = slots_of(list_ref, qi, starts[b] + 4 * g, counts[b], 4)
                merge(state, state, qi, fwd_group(kk, vv, two_heads(qq[qi]), ks, vs))
            return inner

        longest = jnp.maximum(counts[0] - starts[0], counts[1] - starts[1])
        return lax.fori_loop(0, (longest + 3) // 4, body, carry)

    lax.fori_loop(0, ROW, overflow, 0)
    for qi in range(2 * ROW):
        lse_ref[qi] = state[0, qi] + jnp.log(state[1, qi])
        attn_ref[qi * BLOCK : (qi + 1) * BLOCK, :] = (state[2, qi] / state[1, qi]).astype(BF16)
    if not last:
        return
    total = None
    for d, g in enumerate(gos):
        rows = g.shape[0]
        at = pl.ds(pl.multiple_of((r ^ d) * rows, rows), rows)
        part = tn(jnp.concatenate([earlier[at, :], attn_ref[at, :]], axis=1), g[...])
        total = part if total is None else total + part
    if len(terms) == 1:
        terms[0][...] = total.astype(BF16)
        return
    wide[...] = total.astype(BF16)
    half = LANES // 2
    for delta, out in enumerate(terms):
        at = pl.multiple_of((z + delta) % ROW * half, half)
        out[...] = wide[pl.ds(at, half), :]


def far(chunk, fast, lists, own2, rest2, after, state, kk, vv, qq, earlier=None, gos=()):
    last = len(gos) > 0
    width = gos[0].shape[1] if last else LANES
    weights = (jax.ShapeDtypeStruct((LANES // 2, width), BF16),) * ROW
    if not fast:
        weights = (jax.ShapeDtypeStruct((2 * LANES, width), BF16),)
    if not last:
        weights = ()
    more = (earlier, *gos) if last else ()
    return pl.pallas_call(
        functools.partial(far_kernel, chunk, last),
        out_shape=(
            jax.ShapeDtypeStruct(kk.shape, BF16),
            jax.ShapeDtypeStruct(vv.shape, BF16),
            jax.ShapeDtypeStruct((8 * BLOCK, LANES), BF16),
            jax.ShapeDtypeStruct((8, BLOCK, LANES), F32),
        )
        + weights,
        in_specs=[SMEM] + [VMEM] * 2 + [ANY] + [VMEM] * (4 + len(more)),
        out_specs=[VMEM] * (4 + len(weights)),
        input_output_aliases={5: 0, 6: 1},
        scratch_shapes=[
            pltpu.VMEM((3, 8, BLOCK, LANES), F32),
            pltpu.VMEM((2 * LANES, width), BF16),
        ],
        compiler_params=params(),
        cost_estimate=SMALL if last else micros(4.2),
        name=f"far{chunk}",
    )(lists, own2, rest2, after, state, kk, vv, qq, *more)


def bwd_group(kk, vv, q2, g2, lse, delta, ks, vs, diag=None):
    scores = nt(q2, jnp.concatenate([kk[f] for f in ks], axis=0))
    dprob = nt(g2, jnp.concatenate([vv[f, :, 0:LANES] for f in ks], axis=0))
    probs, dscores = [], []
    for i in range(len(ks)):
        part = scores[:, i * BLOCK : (i + 1) * BLOCK]
        if diag == i:
            part = jnp.where(causal(part.shape), part, NEG)
        prob = jnp.exp(part - lse)
        dscores.append((prob * (dprob[:, i * BLOCK : (i + 1) * BLOCK] - delta)).astype(BF16))
        probs.append(prob)
    out = nn(jnp.concatenate(dscores, axis=1), jnp.concatenate([kk[f] for f in vs], axis=0))
    return probs, dscores, out


def back_kernel(chunk, which_d, list_ref, kk, vv, qq, g_ref, attn_ref, lse_ref, after, *refs):
    *outs, dq = refs
    r, _ = place()

    def query_side(qi):
        at = pl.ds(pl.multiple_of(qi * BLOCK, BLOCK), BLOCK)
        g = g_ref[at, chunk * LANES : (chunk + 1) * LANES]
        product = g.astype(F32) * attn_ref[at, :].astype(F32)
        low = low_lanes(product.shape)
        delta = jnp.concatenate(
            [
                jnp.sum(jnp.where(low, product, 0.0), axis=1, keepdims=True),
                jnp.sum(jnp.where(low, 0.0, product), axis=1, keepdims=True),
            ],
            axis=0,
        )
        half = LANES // 2
        lse = jnp.concatenate([lse_ref[qi, :, 0:1], lse_ref[qi, :, half : half + 1]], axis=0)
        return two_heads(qq[qi]), two_heads(g), lse, delta

    for n, d in enumerate(which_d):
        rho = r ^ d
        sides = [query_side(2 * rho + b) for b in (0, 1)]
        local = []
        for b in (0, 1):
            qi = 2 * rho + b
            ks, vs = slots_of(list_ref, qi, 0, list_ref[qi, COUNTS + 1], BACK_FIRST)
            own_ks, own_vs = own_slots(rho, b)
            probs, dscores, add = bwd_group(kk, vv, *sides[b], own_ks + ks, own_vs + vs, diag=1)
            dq[2 * n + b] = add
            local.append(([p.astype(BF16) for p in probs[:2]], dscores[:2]))
        out = outs[n]
        for which, side in ((1, 0), (0, 1)):
            both = jnp.concatenate([sides[0][side], sides[1][side]], axis=0)
            first = jnp.concatenate([local[0][which][1], local[1][which][0]], axis=0)
            base = 512 if side else 256
            out[base : base + BLOCK, :] = tn(first, both).astype(BF16)
            out[base + BLOCK : base + 256, :] = tn(local[1][which][1], sides[1][side]).astype(BF16)

    def overflow(n, carry):
        rho = r ^ ((n + which_d[0]) % ROW)
        counts = [list_ref[2 * rho + b, COUNTS + 1] for b in (0, 1)]

        def body(g, inner):
            for b in (0, 1):
                qi = 2 * rho + b
                ks, vs = slots_of(list_ref, qi, BACK_FIRST + 4 * g, counts[b], 4)
                _, _, add = bwd_group(kk, vv, *query_side(qi), ks, vs)
                dq[2 * n + b] += add
            return inner

        longest = jnp.maximum(counts[0], counts[1])
        return lax.fori_loop(0, (longest - BACK_FIRST + 3) // 4, body, carry)

    lax.fori_loop(0, len(which_d), overflow, 0)
    for n in range(len(which_d)):
        for b in (0, 1):
            outs[n][b * BLOCK : (b + 1) * BLOCK, :] = (pick(dq[2 * n + b]) * 0.125).astype(BF16)


def back(chunk, which_d, lists, kk, vv, qq, grads, attn, lse, after):
    return pl.pallas_call(
        functools.partial(back_kernel, chunk, which_d),
        out_shape=(jax.ShapeDtypeStruct((768, LANES), BF16),) * len(which_d),
        in_specs=[SMEM] + [VMEM] * 6 + [ANY],
        out_specs=[VMEM] * len(which_d),
        scratch_shapes=[pltpu.VMEM((2 * len(which_d), 2 * BLOCK, LANES), F32)],
        compiler_params=params(),
        cost_estimate=SMALL if chunk else micros(8.4),
        name=f"back{chunk}_{which_d[0]}",
    )(lists, kk, vv, qq, grads, attn, lse, after)


def unpack_kernel(chunk, *refs):
    ins, outs = refs[:ROW], refs[-3:]
    r, _ = place()
    odd_me = (r % 2) == 1
    rows, width = outs[0].shape
    for pair in (0, 1):
        tile = (r // 2 + pair) % 2
        first, second = ins[2 * pair], ins[2 * pair + 1]
        for which, out in enumerate(outs):
            a = first[which * rows : (which + 1) * rows, :].astype(F32)
            b = second[which * rows : (which + 1) * rows, :].astype(F32)
            low, high = jnp.where(odd_me, b, a), jnp.where(odd_me, a, b)
            one, two = split_pair(low, high)
            out[:, pl.ds(pl.multiple_of(tile * LANES, LANES), LANES)] = one.astype(BF16)
            out[:, pl.ds(pl.multiple_of((tile + 2) * LANES, LANES), LANES)] = two.astype(BF16)


def unpack(chunk, pieces, rows, width, before):
    half = pl.BlockSpec((rows, width // 2), lambda i: (0, chunk))
    return pl.pallas_call(
        functools.partial(unpack_kernel, chunk),
        grid=(1,),
        out_shape=(jax.ShapeDtypeStruct((rows, width), BF16),) * 3,
        in_specs=[VMEM] * ROW + [ANY] * len(before),
        out_specs=[half] * 3,
        input_output_aliases={ROW + i: i for i in range(len(before))},
        compiler_params=params(),
        cost_estimate=SMALL,
        name=f"unpack{chunk}",
    )(*pieces, *before)


def swap(value, axis, bit):
    count = lax.axis_size(axis)
    return lax.ppermute(value, axis, [(s, s ^ bit) for s in range(count)])


def later(value, axis):
    count = lax.axis_size(axis)
    return lax.ppermute(value, axis, [(s, (s + ROW) % count) for s in range(count)])


hold = lax.optimization_barrier


def shards(queries, keys, values, track, out_weight, grad_out):
    rows, width = queries.shape
    count = lax.axis_size("span")
    fast = count == HEADS

    own0, firsts = pack_first(keys, values)
    own1 = later(own0, "span")
    got_first = [swap(x, "span", d + 1) for d, x in enumerate(firsts)]
    queries, _ = hold((queries, got_first[0]))
    seconds, turns = pack_second(track, queries, keys, values)
    got_first, _ = hold((got_first, seconds[0]))
    rest0 = [stack(2 * rows, got_first)]
    rest1 = [later(rest0[0], "span")]
    seconds, _ = hold((seconds, (rest0[0], own1)))
    got_second = [swap(x, "span", d + 1) for d, x in enumerate(seconds)]
    track_row = jnp.concatenate(
        [track.astype(BF16)] + [x[2 * rows : 2 * rows + 2, : 2 * WINDOW] for x in got_second], axis=0
    )
    lists = plan(track_row.astype(jnp.int32))

    got_second, _ = hold((got_second, rest1[0]))
    rest0.append(stack(2 * rows, got_second))
    turns, _ = hold((turns, (rest0[1], rest1[0])))
    rest1.append(later(rest0[1], "span"))
    own1_late, _ = hold((own1, rest1[1]))
    own2 = later(own1_late, "span")
    turns[1:] = [swap(turns[d], "span", d) for d in (1, 2, 3)]
    grad_late, _ = hold((grad_out, (turns, rest1[1])))
    go2 = swap(grad_late, "span", 2)

    turns, _ = hold((turns, rest1[1]))
    stores = [near(0, lists, own0, rest0[0], own1, rest1[0], turns, lists)]
    stores.append(near(1, lists, own0, rest0[1], own1, rest1[1], turns, stores[0][0]))
    first_row, _ = hold((rest1[0], rest1[1]))
    (second_row, grad_late, go2), _ = hold(((rest1[1], grad_out, go2), stores[1][0]))
    rest2 = [later(first_row, "span"), later(second_row, "span")]
    gos = (grad_out, swap(grad_late, "span", 1), go2, swap(go2, "span", 1))
    grads = grad_attn(out_weight, gos)

    after = stores[1][0]
    kk, vv, attn, lse = far(0, fast, lists, own2, rest2[0], after, *stores[0])
    out = back(0, (0, 1, 2, 3), lists, kk, vv, stores[0][3], grads, attn, lse, attn)
    pieces = [out[0]] + [swap(out[d], "span", d) for d in (1, 2, 3)]

    kk, vv, attn, lse, *terms = far(
        1, fast, lists, own2, rest2[1], out[0], *stores[1], earlier=attn, gos=gos
    )
    second = (lists, kk, vv, stores[1][3], grads, attn, lse)
    if fast:
        weight_grad = terms[0].astype(F32)
        for delta in (1, 2, 3):
            pairs = [
                (ROW * s + q, ROW * ((s + delta) % ROW) + q) for s in range(ROW) for q in range(ROW)
            ]
            weight_grad += lax.ppermute(terms[delta], "span", pairs).astype(F32)
    else:
        head_dim = width // HEADS
        place_in_row = lax.axis_index("span").astype(jnp.int32) % ROW
        mine = terms[0].reshape(ROW, 1, head_dim, width)
        full = jnp.zeros((ROW, ROW, head_dim, width), BF16)
        full = lax.dynamic_update_slice(full, mine, (0, place_in_row, 0, 0)).reshape(width, width)
        weight_grad = lax.psum_scatter(full.astype(F32), "span", scatter_dimension=0, tiled=True)
    out = back(1, (2, 3), *second, attn)
    out, pieces = hold((out, pieces))
    grads_out = unpack(0, pieces, rows, width, ())
    crossed = [swap(x, "span", d) for x, d in zip(out, (2, 3))]
    (beside,) = back(1, (1,), *second, out[0])
    beside = swap(beside, "span", 1)
    (own,) = back(1, (0,), *second, out[1])
    pieces = [own, beside] + crossed
    query_grad, key_grad, value_grad = unpack(1, pieces, rows, width, grads_out)
    return (query_grad, key_grad, value_grad, weight_grad)


def solution(mesh):
    spec = P(("groups", "span"), None)
    return jax.shard_map(
        shards,
        mesh=mesh,
        in_specs=(spec, spec, spec, spec, P(), spec),
        out_specs=(spec, spec, spec, spec),
        check_vma=False,
    )
```
